32 devices in a mesh: ctx: 8 (over z, x), ch: 4 (over y, core).
Axes of the slice: x: 2, y: 2, z: 4, core: 2. Of those that a mesh axis runs over, the one named last changes fastest.
Arguments:
- x_first: bfloat16 [4096, 2048], P('ch', 'ctx'), may hold values from -6 to 6
- x_second: bfloat16 [4096, 2048], P('ch', 'ctx'), may hold values from -6 to 6
- x_value: bfloat16 [4096, 2048], P('ch', 'ctx'), may hold values from -6 to 6
- short_filter: float32 [3, 3, 4096], P(None, None, 'ch'), may hold values from -4 to 4
- long_filter: bfloat16 [4096, 2048], P('ch', 'ctx'), may hold values from -0.125 to 0.125
- skip_bias: float32 [4096], P('ch'), may hold values from -4 to 4
- norm_gain: float32 [4096], P('ch'), may hold values from 0.1 to 1.9
- cotangent: bfloat16 [4096, 2048], P('ch', 'ctx'), may hold values from -6 to 6
Outputs:
- output: bfloat16 [4096, 2048], P('ch', 'ctx')
- d_first: bfloat16 [4096, 2048], P('ch', 'ctx')
- d_second: bfloat16 [4096, 2048], P('ch', 'ctx')
- d_value: bfloat16 [4096, 2048], P('ch', 'ctx')
- d_long: float32 [4096, 2048], P(('ch', 'ctx'))
- d_short: float32 [3, 3, 4096], P(None, None, ('ch', 'ctx'))
- d_bias: float32 [4096], P(('ch', 'ctx'))
- d_gain: float32 [4096], P(('ch', 'ctx'))
The draws below stay inside these ranges and needn't reach their ends.
All inputs are finite; a program needn't handle non-finite values.
Results may differ from the reference program's by a relative error of at most 0.012.
Values may be sent and summed in bfloat16 or wider, within the bound.
No kernel may reach another device: no remote copies, remote signals or barrier semaphores. Data moves between devices by JAX's collectives and lax.ppermute only.
A program may use at most 128 MiB of HBM per device.

```python
import jax
import jax.numpy as jnp
from jax import lax

D = 4096
LENGTH = 2048


def steps_of(key, dims, cuts, smallest, top_value):
    gain, own = 1.0, jax.random.fold_in(key, 6)
    for position, shards_of in cuts:
        steps = jnp.exp(jax.random.uniform(jax.random.fold_in(own, position), (shards_of,), jnp.float32, smallest / len(cuts), top_value / len(cuts)))
        gain = gain * jnp.repeat(steps, dims[position] // shards_of).reshape([-1 if axis == position else 1 for axis in range(len(dims))])
    return gain


def bell_draw(key, dims, width, bound, cuts=(), kind=jnp.bfloat16):
    values = width * jax.random.normal(key, dims, jnp.float32)
    if cuts:
        values = values * steps_of(key, dims, cuts, -0.22, 0.18)
    return jnp.clip(values, -bound, bound).astype(kind)


def setup_inputs(seed: int = 0) -> dict:
    key_of = jax.random.split(jax.random.key(seed), 9)
    return {
        "x_first": bell_draw(key_of[0], (D, LENGTH), 1.0, 6.0, ((0, 4), (1, 8))),
        "x_second": bell_draw(key_of[1], (D, LENGTH), 1.0, 6.0, ((0, 4), (1, 8))),
        "x_value": bell_draw(key_of[2], (D, LENGTH), 1.0, 6.0, ((0, 4), (1, 8))),
        "short_filter": bell_draw(key_of[3], (3, 3, D), 0.6, 4.0, ((2, 4),), jnp.float32),
        "long_filter": bell_draw(key_of[4], (D, LENGTH), LENGTH ** -0.5, 0.125, ((0, 4), (1, 8))),
        "skip_bias": bell_draw(key_of[5], (D,), 1.0, 4.0, ((0, 4),), jnp.float32),
        "norm_gain": jnp.clip(1.0 + 0.18 * jax.random.normal(key_of[6], (D,), jnp.float32), 0.1, 1.9),
        "cotangent": bell_draw(key_of[7], (D, LENGTH), 1.0, 6.0, ((0, 4), (1, 8))),
    }


EPS = 1e-06

def short_forward(values, taps):
    padded = jnp.pad(values.astype(jnp.float32), ((0, 0), (2, 0)))
    return taps[0][:, None] * padded[:, 2:] + taps[1][:, None] * padded[:, 1:-1] + taps[2][:, None] * padded[:, :-2]

def short_adjoint(grads, taps):
    padded = jnp.pad(grads.astype(jnp.float32), ((0, 0), (0, 2)))
    return taps[0][:, None] * padded[:, :-2] + taps[1][:, None] * padded[:, 1:-1] + taps[2][:, None] * padded[:, 2:]

def blocked(array, block):
    return array.reshape(array.shape[0] // block, block, array.shape[1])

def reference(x_first, x_second, x_value, short_filter, long_filter, skip_bias, norm_gain, cotangent):
    total = 2 * LENGTH
    block = min(256, D)
    inputs = [x_first, x_second, x_value]
    shorts = [short_forward(inputs[b], short_filter[b]).astype(jnp.bfloat16) for b in range(3)]
    gated = (shorts[1].astype(jnp.float32) * shorts[2].astype(jnp.float32)).astype(jnp.bfloat16)

    def convolve(pair):
        gate_part, filt_part = pair
        spec = jnp.fft.rfft(gate_part.astype(jnp.float32), n=total, axis=-1) * jnp.fft.rfft(filt_part.astype(jnp.float32), n=total, axis=-1)
        return jnp.fft.irfft(spec, n=total, axis=-1)[:, :LENGTH].astype(jnp.bfloat16)
    conv = lax.map(convolve, (blocked(gated, block), blocked(long_filter, block))).reshape(D, LENGTH)
    inner = conv.astype(jnp.float32) + skip_bias[:, None] * gated.astype(jnp.float32)
    mixed = shorts[0].astype(jnp.float32) * inner
    recip = lax.rsqrt(lax.optimization_barrier(jnp.mean(mixed * mixed, axis=0)) + EPS)
    output = (mixed * recip * norm_gain[:, None]).astype(jnp.bfloat16)
    scaled = cotangent.astype(jnp.float32) * norm_gain[:, None]
    dotted = lax.optimization_barrier(jnp.sum(scaled * mixed, axis=0))
    d_mixed = recip * scaled - mixed * recip ** 3 * (dotted / D)
    d_inner = (d_mixed * shorts[0].astype(jnp.float32)).astype(jnp.bfloat16)
    grad_first = (d_mixed * inner).astype(jnp.bfloat16)
    d_gain = lax.optimization_barrier(jnp.sum(cotangent.astype(jnp.float32) * mixed * recip, axis=1))
    d_bias = lax.optimization_barrier(jnp.sum(d_inner.astype(jnp.float32) * gated.astype(jnp.float32), axis=1))

    def correlate(triple):
        gate_part, filt_part, grad_part = triple
        gate_spec = jnp.fft.rfft(gate_part.astype(jnp.float32), n=total, axis=-1)
        filt_spec = jnp.fft.rfft(filt_part.astype(jnp.float32), n=total, axis=-1)
        grad_spec = jnp.fft.rfft(grad_part.astype(jnp.float32), n=total, axis=-1)
        back_part = jnp.fft.irfft(jnp.conj(filt_spec) * grad_spec, n=total, axis=-1)[:, :LENGTH].astype(jnp.bfloat16)
        long_part = jnp.fft.irfft(jnp.conj(gate_spec) * grad_spec, n=total, axis=-1)[:, :LENGTH]
        return (back_part, long_part)
    back, d_long = lax.map(correlate, (blocked(gated, block), blocked(long_filter, block), blocked(d_inner, block)))
    back = back.reshape(D, LENGTH)
    d_long = d_long.reshape(D, LENGTH)
    d_gated = (skip_bias[:, None] * d_inner.astype(jnp.float32) + back.astype(jnp.float32)).astype(jnp.bfloat16)
    grad_second = (d_gated.astype(jnp.float32) * shorts[2].astype(jnp.float32)).astype(jnp.bfloat16)
    grad_third = (d_gated.astype(jnp.float32) * shorts[1].astype(jnp.float32)).astype(jnp.bfloat16)
    grads = [grad_first, grad_second, grad_third]
    d_inputs = [short_adjoint(grads[b], short_filter[b]).astype(jnp.bfloat16) for b in range(3)]
    rows = []
    for b in range(3):
        padded = jnp.pad(inputs[b].astype(jnp.float32), ((0, 0), (2, 0)))
        gradf = grads[b].astype(jnp.float32)
        rows.append(jnp.stack([lax.optimization_barrier(jnp.sum(gradf * padded[:, 2 - k:2 - k + LENGTH], axis=1)) for k in range(3)]))
    d_short = jnp.stack(rows)
    return (output, d_inputs[0], d_inputs[1], d_inputs[2], d_long, d_short, d_bias, d_gain)
```

```python
import math

import jax
import jax.numpy as jnp
import numpy as np
from jax import lax
from jax.experimental import pallas as pl
from jax.experimental.pallas import tpu as pltpu
from jax.sharding import PartitionSpec as P

EPS = 1e-06
LANES = 128
ROWS = 16
HALF = 8


def shifted(value, axis, steps):
    count = lax.axis_size(axis)
    first, last = (max(0, -steps), min(count, count - steps))
    return lax.ppermute(value, axis, [(source, source + steps) for source in range(first, last)])


def root(angle):
    return math.cos(2 * math.pi * angle), math.sin(2 * math.pi * angle)


def slab_angles(slabs):
    angles = [-0.25]
    while len(angles) < slabs:
        angles = [a / 2 + extra for a in angles for extra in (0.0, 0.5)]
    return angles


def split_angles(slabs):
    levels, angles = [], [-0.25]
    while len(angles) < slabs:
        levels.append([a / 2 for a in angles])
        angles = [a / 2 + extra for a in angles for extra in (0.0, 0.5)]
    return levels


def slabs_forward(xs):
    slabs = len(xs)
    data = None
    for level, turns in enumerate(split_angles(slabs)):
        size = slabs >> level
        half = size // 2
        new = [None] * slabs
        for b, turn in enumerate(turns):
            c, s = root(turn)
            for n in range(half):
                lo, hi = b * size + n, b * size + n + half
                if data is None:
                    tr, ti = xs[hi] * c, xs[hi] * s
                    new[lo] = (xs[lo] + tr, ti)
                    new[hi] = (xs[lo] - tr, -ti)
                else:
                    (ar, ai), (br, bi) = data[lo], data[hi]
                    tr, ti = br * c - bi * s, br * s + bi * c
                    new[lo] = (ar + tr, ai + ti)
                    new[hi] = (ar - tr, ai - ti)
        data = new
    return data


def slabs_inverse(data):
    slabs = len(data)
    levels = split_angles(slabs)
    for level in range(len(levels) - 1, -1, -1):
        size = slabs >> level
        half = size // 2
        new = [None] * slabs
        for b, turn in enumerate(levels[level]):
            c, s = root(turn)
            for n in range(half):
                lo, hi = b * size + n, b * size + n + half
                (ur, ui), (vr, vi) = data[lo], data[hi]
                dr, di = ur - vr, ui - vi
                if level == 0:
                    new[lo] = ur + vr
                    new[hi] = dr * c + di * s
                else:
                    new[lo] = (ur + vr, ui + vi)
                    new[hi] = (dr * c + di * s, di * c - dr * s)
        data = new
    return data


def make_tables(length):
    slabs = length // LANES
    angle = np.array(slab_angles(slabs))[:, None] * np.arange(LANES)[None, :] / LANES
    twist = np.stack([np.cos(2 * np.pi * angle), np.sin(2 * np.pi * angle)], 1).astype(np.float32)
    grid = np.arange(LANES)[:, None] * np.arange(LANES)[None, :] % LANES * (2 * np.pi / LANES)
    cos, sin = np.cos(grid), np.sin(grid)
    fwd = np.block([[cos, -sin], [sin, cos]]).astype(np.float32)
    inv = np.block([[cos, sin], [-sin, cos]]).astype(np.float32)

    def two(mat):
        upper = mat.astype(jnp.bfloat16)
        lower = (mat - upper.astype(np.float32)).astype(jnp.bfloat16)
        return np.stack([upper, lower])

    return jnp.asarray(twist), jnp.asarray(two(fwd)), jnp.asarray(two(inv))


def split_dot(value, mat_ref):
    upper = value.astype(jnp.bfloat16)
    lower = (value - upper.astype(jnp.float32)).astype(jnp.bfloat16)
    dot = lambda a, b: jnp.dot(a, b, preferred_element_type=jnp.float32)
    return dot(upper, mat_ref[0]) + (dot(lower, mat_ref[0]) + dot(upper, mat_ref[1]))


def forward_group(x_ref, row, twist_ref, mat_ref, work):
    parts, _, width = x_ref.shape
    per = width // LANES
    slabs = parts * per
    xs = [
        x_ref[s // per, row : row + ROWS, s % per * LANES : (s % per + 1) * LANES].astype(jnp.float32)
        for s in range(slabs)
    ]
    for h in range(0, ROWS, HALF):
        data = slabs_forward([x[h : h + HALF] for x in xs])
        for j, (re, im) in enumerate(data):
            tc, ts = twist_ref[j, 0:1], twist_ref[j, 1:2]
            work[j * ROWS + h : j * ROWS + h + HALF, :LANES] = re * tc - im * ts
            work[j * ROWS + h : j * ROWS + h + HALF, LANES:] = re * ts + im * tc
    return split_dot(work[...], mat_ref)


def inverse_group(spec, scale, twist_ref, mat_ref, work, store):
    slabs = spec.shape[0] // ROWS
    work[...] = split_dot(spec * scale, mat_ref)
    for h in range(0, ROWS, HALF):
        data = []
        for j in range(slabs):
            tc, ts = twist_ref[j, 0:1], twist_ref[j, 1:2]
            re = work[j * ROWS + h : j * ROWS + h + HALF, :LANES]
            im = work[j * ROWS + h : j * ROWS + h + HALF, LANES:]
            data.append((re * tc + im * ts, im * tc - re * ts))
        for s, value in enumerate(slabs_inverse(data)):
            store(s, h, value)


def product(a, b):
    ar, ai, br, bi = a[:, :LANES], a[:, LANES:], b[:, :LANES], b[:, LANES:]
    return jnp.concatenate([ar * br - ai * bi, ar * bi + ai * br], 1)


def conj_product(a, b):
    ar, ai, br, bi = a[:, :LANES], a[:, LANES:], b[:, :LANES], b[:, LANES:]
    return jnp.concatenate([ar * br + ai * bi, ar * bi - ai * br], 1)


def spectrum_kernel(x_ref, twist_ref, mat_ref, spec_ref, work):
    for g in range(spec_ref.shape[0]):
        spec_ref[g] = forward_group(x_ref, g * ROWS, twist_ref, mat_ref, work.at[g])


def filter_kernel(conj, scale, x_ref, filt_ref, twist_ref, fwd_ref, inv_ref, out_ref, spec_ref, work, outs):
    per = x_ref.shape[2] // LANES
    for g in range(spec_ref.shape[0]):
        spec = forward_group(x_ref, g * ROWS, twist_ref, fwd_ref, work.at[g])
        spec_ref[g] = spec
        mixed = (conj_product if conj else product)(filt_ref[g], spec)

        def store(s, h, value):
            outs[g, s, h : h + HALF] = value

        inverse_group(mixed, scale, twist_ref, inv_ref, work.at[g], store)
        for s in range(outs.shape[1]):
            out_ref[s // per, g * ROWS : (g + 1) * ROWS, s % per * LANES : (s % per + 1) * LANES] = outs[g, s].astype(
                out_ref.dtype
            )


def lags_kernel(scale, gate_ref, grad_ref, twist_ref, inv_ref, out_ref, work):
    for g in range(gate_ref.shape[0]):

        def store(s, h, value):
            out_ref[g * ROWS + h : g * ROWS + h + HALF, s * LANES : (s + 1) * LANES] = value

        inverse_group(conj_product(gate_ref[g], grad_ref[g]), scale, twist_ref, inv_ref, work.at[g], store)


def transforms(parts, chans, width):
    length = parts * width
    slabs = length // LANES
    groups = chans // ROWS
    per = 2 if groups % 2 == 0 else 1
    grid = (groups // per,)
    twist, fwd, inv = make_tables(length)
    scale = 1.0 / length
    x_spec = pl.BlockSpec((parts, per * ROWS, width), lambda i: (0, i, 0))
    s_spec = pl.BlockSpec((per, slabs * ROWS, 2 * LANES), lambda i: (i, 0, 0))
    l_spec = pl.BlockSpec((per * ROWS, length), lambda i: (i, 0))
    t_spec = pl.BlockSpec(twist.shape, lambda i: (0, 0, 0))
    m_spec = pl.BlockSpec(fwd.shape, lambda i: (0, 0, 0))
    s_shape = jax.ShapeDtypeStruct((groups, slabs * ROWS, 2 * LANES), jnp.float32)
    work = pltpu.VMEM((per, slabs * ROWS, 2 * LANES), jnp.float32)
    outs = pltpu.VMEM((per, slabs, ROWS, LANES), jnp.float32)
    params = pltpu.CompilerParams(vmem_limit_bytes=48 * 2**20)
    flops = 2 * 3 * groups * slabs * ROWS * 256 * 256
    cost = lambda n: pl.CostEstimate(flops=n * flops * 4, bytes_accessed=6 * 2**20, transcendentals=0)

    def spectrum(x):
        return pl.pallas_call(
            spectrum_kernel,
            grid=grid,
            in_specs=[x_spec, t_spec, m_spec],
            out_specs=s_spec,
            out_shape=s_shape,
            scratch_shapes=[work],
            compiler_params=params,
            cost_estimate=cost(1),
            name="spectrum",
        )(x, twist, fwd)

    def apply(x, filt, conj):
        return pl.pallas_call(
            lambda *refs: filter_kernel(conj, scale, *refs),
            grid=grid,
            in_specs=[x_spec, s_spec, t_spec, m_spec, m_spec],
            out_specs=(x_spec, s_spec),
            out_shape=(jax.ShapeDtypeStruct(x.shape, jnp.bfloat16), s_shape),
            scratch_shapes=[work, outs],
            compiler_params=params,
            cost_estimate=cost(2),
            name="correlate" if conj else "convolve",
        )(x, filt, twist, fwd, inv)

    def lags(gate, grad):
        return pl.pallas_call(
            lambda *refs: lags_kernel(scale, *refs),
            grid=grid,
            in_specs=[s_spec, s_spec, t_spec, m_spec],
            out_specs=l_spec,
            out_shape=jax.ShapeDtypeStruct((chans, length), jnp.float32),
            scratch_shapes=[work],
            compiler_params=params,
            cost_estimate=cost(1),
            name="lags",
        )(gate, grad, twist, inv)

    return spectrum, apply, lags


def exchange(value):
    return lax.all_to_all(value, "ctx", split_axis=0, concat_axis=0, tiled=True)


def scatter_sum(value):
    count = lax.axis_size("ctx")
    me = lax.axis_index("ctx")
    bit = 1
    while bit < count:
        pairs = value.reshape((value.shape[0] // 2, 2) + value.shape[1:])
        mine = me // bit % 2
        keep = lax.dynamic_index_in_dim(pairs, mine, 1, False)
        send = lax.dynamic_index_in_dim(pairs, 1 - mine, 1, False)
        value = keep + lax.ppermute(send, "ctx", [(i, i ^ bit) for i in range(count)])
        bit *= 2
    return value[0]


def local(x_first, x_second, x_value, short_filter, long_filter, skip_bias, norm_gain, cotangent):
    chans, steps_dev = x_first.shape
    n_ctx = lax.axis_size("ctx")
    n_ch = lax.axis_size("ch")
    width = chans * n_ch
    own = chans // n_ctx
    spectrum, apply, lags = transforms(n_ctx, own, steps_dev)
    f32 = lambda v: v.astype(jnp.float32)
    bf16 = lambda v: v.astype(jnp.bfloat16)
    by_dev = lambda v: v.reshape(n_ctx, own, steps_dev)
    by_pos = lambda v: v.reshape(chans, steps_dev)

    filter_cm = exchange(by_dev(long_filter))
    inputs = jnp.stack([x_first, x_second, x_value])
    before = shifted(inputs[:, :, steps_dev - 2 :], "ctx", 1)
    padded = f32(jnp.concatenate([before, inputs], axis=2))
    taps = short_filter[:, :, :, None]
    shorts = bf16(taps[:, 0] * padded[:, :, 2:] + taps[:, 1] * padded[:, :, 1:-1] + taps[:, 2] * padded[:, :, :-2])
    first_s, second_s, third_s = shorts[0], shorts[1], shorts[2]
    gated = bf16(f32(second_s) * f32(third_s))
    bias_col = skip_bias[:, None]
    gain_col = norm_gain[:, None]
    gated_cm = exchange(by_dev(gated))
    filt_spec = spectrum(filter_cm)
    conv_cm, gate_spec = apply(gated_cm, filt_spec, False)
    conv = by_pos(exchange(conv_cm))
    inner = f32(conv) + bias_col * f32(gated)
    mixed = f32(first_s) * inner
    scaled = f32(cotangent) * gain_col
    sums = jnp.stack([jnp.sum(mixed * mixed, axis=0), jnp.sum(scaled * mixed, axis=0)])
    total = sums
    for k in range(1, n_ch):
        total = total + lax.ppermute(sums, "ch", [(i, (i + k) % n_ch) for i in range(n_ch)])
    sum_sq, dotted = total[0], total[1]
    recip = lax.rsqrt(sum_sq / width + EPS)
    output = bf16(mixed * recip * gain_col)
    d_mixed = recip * scaled - mixed * recip**3 * (dotted / width)
    d_inner = bf16(d_mixed * f32(first_s))
    d_inner_cm = exchange(by_dev(d_inner))
    grad_first = bf16(d_mixed * inner)
    gain_part = jnp.sum(f32(cotangent) * mixed * recip, axis=1)
    bias_part = jnp.sum(f32(d_inner) * f32(gated), axis=1)
    back_cm, grad_spec = apply(d_inner_cm, filt_spec, True)
    back = by_pos(exchange(back_cm))
    d_long = lags(gate_spec, grad_spec)
    d_gated = bf16(bias_col * f32(d_inner) + f32(back))
    grad_second = bf16(f32(d_gated) * f32(third_s))
    grad_third = bf16(f32(d_gated) * f32(second_s))
    grads = jnp.stack([grad_first, grad_second, grad_third])
    after = shifted(grads[:, :, :2], "ctx", -1)
    grad_pad = f32(jnp.concatenate([grads, after], axis=2))
    d_inputs = bf16(
        taps[:, 0] * grad_pad[:, :, :-2] + taps[:, 1] * grad_pad[:, :, 1:-1] + taps[:, 2] * grad_pad[:, :, 2:]
    )
    grads_f = f32(grads)
    parts = [jnp.sum(grads_f * padded[:, :, 2 - k : 2 - k + steps_dev], axis=2) for k in range(3)]
    rows = jnp.concatenate([jnp.concatenate(parts, 0), bias_part[None], gain_part[None]], 0)
    rows = rows.reshape(11, n_ctx, own).transpose(1, 0, 2)
    done = scatter_sum(rows)
    d_short = done[:9].reshape(3, 3, own).transpose(1, 0, 2)
    return (output, d_inputs[0], d_inputs[1], d_inputs[2], d_long, d_short, done[9], done[10])


def solution(mesh):
    seq = P("ch", "ctx")
    own = ("ch", "ctx")
    return jax.shard_map(
        local,
        mesh=mesh,
        in_specs=(seq, seq, seq, P(None, None, "ch"), seq, P("ch"), P("ch"), seq),
        out_specs=(seq, seq, seq, seq, P(own, None), P(None, None, own), P(own), P(own)),
        check_vma=False,
    )
```

```python
import math

import jax
import jax.numpy as jnp
import numpy as np
from jax import lax
from jax.experimental import pallas as pl
from jax.experimental.pallas import tpu as pltpu
from jax.sharding import PartitionSpec as P

EPS = 1e-06
LANES = 128
ROWS = 16
HALF = 8
VMEM_MOST = 24 * 2**20
VMEM_ALL = 60 * 2**20
PARTS = 4


def f32(value):
    return value.astype(jnp.float32)


def bf16(value):
    return value.astype(jnp.bfloat16)


def shifted(value, axis, steps):
    count = lax.axis_size(axis)
    first, last = (max(0, -steps), min(count, count - steps))
    return lax.ppermute(value, axis, [(source, source + steps) for source in range(first, last)])


def root(angle):
    return math.cos(2 * math.pi * angle), math.sin(2 * math.pi * angle)


def slab_angles(slabs):
    angles = [-0.25]
    while len(angles) < slabs:
        angles = [a / 2 + extra for a in angles for extra in (0.0, 0.5)]
    return angles


def split_angles(slabs):
    levels, angles = [], [-0.25]
    while len(angles) < slabs:
        levels.append([a / 2 for a in angles])
        angles = [a / 2 + extra for a in angles for extra in (0.0, 0.5)]
    return levels


def slabs_forward(xs):
    slabs = len(xs)
    data = None
    for level, turns in enumerate(split_angles(slabs)):
        size = slabs >> level
        half = size // 2
        new = [None] * slabs
        for b, turn in enumerate(turns):
            c, s = root(turn)
            for n in range(half):
                lo, hi = b * size + n, b * size + n + half
                if data is None:
                    tr, ti = xs[hi] * c, xs[hi] * s
                    new[lo] = (xs[lo] + tr, ti)
                    new[hi] = (xs[lo] - tr, -ti)
                else:
                    (ar, ai), (br, bi) = data[lo], data[hi]
                    tr, ti = br * c - bi * s, br * s + bi * c
                    new[lo] = (ar + tr, ai + ti)
                    new[hi] = (ar - tr, ai - ti)
        data = new
    return data


def slabs_inverse(data):
    slabs = len(data)
    levels = split_angles(slabs)
    for level in range(len(levels) - 1, -1, -1):
        size = slabs >> level
        half = size // 2
        new = [None] * slabs
        for b, turn in enumerate(levels[level]):
            c, s = root(turn)
            for n in range(half):
                lo, hi = b * size + n, b * size + n + half
                (ur, ui), (vr, vi) = data[lo], data[hi]
                dr, di = ur - vr, ui - vi
                if level == 0:
                    new[lo] = ur + vr
                    new[hi] = dr * c + di * s
                else:
                    new[lo] = (ur + vr, ui + vi)
                    new[hi] = (dr * c + di * s, di * c - dr * s)
        data = new
    return data


def make_tables(length):
    slabs = length // LANES
    angle = np.array(slab_angles(slabs))[:, None] * np.arange(LANES)[None, :] / LANES
    twist = np.stack([np.cos(2 * np.pi * angle), np.sin(2 * np.pi * angle)], 1).astype(np.float32)
    grid = np.arange(LANES)[:, None] * np.arange(LANES)[None, :] % LANES * (2 * np.pi / LANES)
    cos, sin = np.cos(grid), np.sin(grid)
    fwd = np.block([[cos, -sin], [sin, cos]]).astype(np.float32)
    inv = np.block([[cos, sin], [-sin, cos]]).astype(np.float32)

    def two(mat):
        upper = mat.astype(jnp.bfloat16)
        lower = (mat - upper.astype(np.float32)).astype(jnp.bfloat16)
        return np.stack([upper, lower])

    return jnp.asarray(np.stack([twist, twist / length])), jnp.asarray(two(fwd)), jnp.asarray(two(inv))


def split_dot(value, mat_ref):
    upper = value.astype(jnp.bfloat16)
    lower = (value - upper.astype(jnp.float32)).astype(jnp.bfloat16)
    dot = lambda a, b: jnp.dot(a, b, preferred_element_type=jnp.float32)
    return dot(upper, mat_ref[0]) + (dot(lower, mat_ref[0]) + dot(upper, mat_ref[1]))


def forward_group(x_ref, row, twist_ref, mat_ref, work):
    parts, _, width = x_ref.shape
    per = width // LANES
    slabs = parts * per
    xs = [f32(x_ref[s // per, pl.ds(row, ROWS), s % per * LANES : (s % per + 1) * LANES]) for s in range(slabs)]
    for h in range(0, ROWS, HALF):
        data = slabs_forward([x[h : h + HALF] for x in xs])
        for j, (re, im) in enumerate(data):
            tc, ts = twist_ref[j, 0:1], twist_ref[j, 1:2]
            work[j * ROWS + h : j * ROWS + h + HALF, :LANES] = re * tc - im * ts
            work[j * ROWS + h : j * ROWS + h + HALF, LANES:] = re * ts + im * tc
    return split_dot(work[...], mat_ref)


def inverse_group(spec, twist_ref, mat_ref, work, store):
    slabs = spec.shape[0] // ROWS
    work[...] = split_dot(spec, mat_ref)
    for h in range(0, ROWS, HALF):
        data = []
        for j in range(slabs):
            tc, ts = twist_ref[j, 0:1], twist_ref[j, 1:2]
            re = work[j * ROWS + h : j * ROWS + h + HALF, :LANES]
            im = work[j * ROWS + h : j * ROWS + h + HALF, LANES:]
            data.append((re * tc + im * ts, im * tc - re * ts))
        for s, value in enumerate(slabs_inverse(data)):
            store(s, h, value)


def product(a, b):
    ar, ai, br, bi = a[:, :LANES], a[:, LANES:], b[:, :LANES], b[:, LANES:]
    return jnp.concatenate([ar * br - ai * bi, ar * bi + ai * br], 1)


def conj_product(a, b):
    ar, ai, br, bi = a[:, :LANES], a[:, LANES:], b[:, :LANES], b[:, LANES:]
    return jnp.concatenate([ar * br + ai * bi, ar * bi - ai * br], 1)


def spectrum_pair(filt_ref, gate_ref, row, twist_ref, fwd_ref, work):
    one = forward_group(filt_ref, row, twist_ref.at[0], fwd_ref, work.at[0])
    return one, forward_group(gate_ref, row, twist_ref.at[0], fwd_ref, work.at[1])


def put_slabs(out_ref, row, slabs_ref):
    per = out_ref.shape[2] // LANES
    for s in range(slabs_ref.shape[0]):
        lanes = slice(s % per * LANES, (s % per + 1) * LANES)
        out_ref[s // per, pl.ds(row, ROWS), lanes] = bf16(slabs_ref[s])


def storing(slabs_ref):
    def store(s, h, value):
        slabs_ref[s, h : h + HALF] = value

    return store


def over_groups(count, per, body, done):
    def step(i, carry):
        for g in range(per):
            body(g, pl.multiple_of((i * per + g) * ROWS, ROWS))
        done(i)
        return carry

    lax.fori_loop(0, count // per, step, 0)


def column(cols_ref, rows, k):
    return cols_ref[rows, k : k + 1]


def tap(cols_ref, rows, branch, k):
    return column(cols_ref, rows, 3 * branch + k)


BIAS, GAIN = 9, 10


def after_wrap(now, before, steps):
    lanes = lax.broadcasted_iota(jnp.int32, now.shape, 1)
    return jnp.where(lanes < steps, before, now)


def short_slabs(x_ref, row, taps):
    parts, _, width = x_ref.shape
    per = width // LANES
    result, last = [], [0.0, 0.0]
    for s in range(parts * per):
        x = f32(x_ref[s // per, pl.ds(row, ROWS), s % per * LANES : (s % per + 1) * LANES])
        moved = [pltpu.roll(x, k, 1) for k in (1, 2)]
        one, two = (after_wrap(moved[k], last[k], k + 1) for k in range(2))
        result.append(bf16(taps[0] * x + taps[1] * one + taps[2] * two))
        last = moved
    return result


def convolve_kernel(pack_ref, cols_ref, twist_ref, fwd_ref, inv_ref, out_ref, spec_ref, gate_ref, token_ref, work, slabs, sent):
    chans = out_ref.shape[1]
    per = out_ref.shape[2] // LANES
    filt_ref, x1_ref, x2_ref = (pack_ref.at[:, k * chans : (k + 1) * chans] for k in range(3))

    def body(g, row):
        rows = pl.ds(row, ROWS)
        s1, s2 = (
            short_slabs(ref, row, [tap(cols_ref, rows, b, k) for k in range(3)]) for b, ref in ((1, x1_ref), (2, x2_ref))
        )
        for s, (one, two) in enumerate(zip(s1, s2)):
            gate_ref[s // per, rows, s % per * LANES : (s % per + 1) * LANES] = bf16(f32(one) * f32(two))
        filt, gate = spectrum_pair(filt_ref, gate_ref, row, twist_ref, fwd_ref, work.at[g])
        spec_ref[row // ROWS] = filt
        inverse_group(product(filt, gate), twist_ref.at[1], inv_ref, work.at[g, 0], storing(slabs.at[g]))
        put_slabs(out_ref, row, slabs.at[g])

    over_groups(chans // ROWS, work.shape[0], body, sent)
    token_ref[...] = jnp.zeros_like(token_ref)


def correlate_kernel(grad_ref, spec_ref, early_ref, twist_ref, fwd_ref, inv_ref, out_ref, work, slabs, sent):
    parts, chans, width = grad_ref.shape
    groups, per = chans // ROWS, work.shape[0]

    def body(g, row):
        grad = forward_group(grad_ref, row, twist_ref.at[0], fwd_ref, work.at[g, 0])
        mixed = conj_product(spec_ref[row // ROWS], grad)
        inverse_group(mixed, twist_ref.at[1], inv_ref, work.at[g, 0], storing(slabs.at[g]))
        put_slabs(out_ref, row, slabs.at[g])

    def done(i):
        for g in range(per):
            sent(i * per + g)

    over_groups(groups, per, body, done)
    for part in range(parts):
        sums = early_ref[:4, part * chans : (part + 1) * chans]
        upper = f32(bf16(sums))
        if part + 1 < parts:
            tips = to_rows([(0, 0), (1, 1), (2, 0), (3, 1)], out_ref[part + 1, :chans, :LANES])[:4]
        else:
            tips = jnp.zeros((4, chans), jnp.float32)
        rows = jnp.concatenate([tips, upper, sums - upper, jnp.zeros((4, chans), jnp.float32)], 0)
        rows = jnp.concatenate([rows, jnp.zeros((ROWS, width - chans), jnp.float32)], 1)
        out_ref[part, chans:] = bf16(rows)
    sent(groups)


def grads_kernel(back_ref, inner_ref, pack_ref, gate_ref, cols_ref, rows_ref, tiles, sent):
    parts, chans, _ = inner_ref.shape
    block = min(32, chans)
    for row in range(0, chans, block):
        rows = slice(row, row + block)
        taps = [[tap(cols_ref, rows, b, k) for k in range(3)] for b in range(3)]
        bias = column(cols_ref, rows, BIAS)
        totals, last = [None] * 7, [[None] * 2, [None] * 2]
        for part in range(parts):
            moved, shorts = [], []
            for b in (1, 2):
                x = f32(pack_ref[part, b * chans + row : b * chans + row + block])
                turns = [pltpu.roll(x, k, 1) for k in (1, 2)]
                fixed = []
                for k in range(2):
                    before = 0.0 if part == 0 else last[b - 1][k]
                    head = after_wrap(turns[k][:, :LANES], before, k + 1)
                    fixed.append(jnp.concatenate([head, turns[k][:, LANES:]], 1))
                    last[b - 1][k] = turns[k][:, :LANES]
                moved.append([x] + fixed)
                shorts.append(f32(bf16(taps[b][0] * x + taps[b][1] * fixed[0] + taps[b][2] * fixed[1])))
            inner = f32(inner_ref[part, rows])
            d_gated = f32(bf16(bias * inner + f32(back_ref[part, rows])))
            terms = []
            for b in (1, 2):
                g = f32(bf16(d_gated * shorts[2 - b]))
                terms += [fold(g * moved[b - 1][k]) for k in range(3)]
            terms.append(fold(inner * f32(gate_ref[part, rows])))
            totals = [t if total is None else total + t for total, t in zip(totals, terms)]
        for k in range(7):
            tiles[k, rows] = totals[k]
    rows_ref[...] = sum([sum_rows(k, tiles.at[k]) for k in range(7)])[:8]


def lags_kernel(gate_ref, grad_ref, twist_ref, fwd_ref, inv_ref, out_ref, token_ref, work, sent):
    chans = out_ref.shape[0]
    def body(g, row):
        def store(s, h, value):
            out_ref[pl.ds(pl.multiple_of(row + h, HALF), HALF), s * LANES : (s + 1) * LANES] = value

        gate, grad = spectrum_pair(gate_ref, grad_ref, row, twist_ref, fwd_ref, work.at[g])
        inverse_group(conj_product(gate, grad), twist_ref.at[1], inv_ref, work.at[g, 0], store)

    over_groups(chans // ROWS, work.shape[0], body, sent)
    token_ref[...] = jnp.zeros_like(token_ref)


def place(kernel, name, outs, args, scratch=(), flops=10**6, after=(), vmem=VMEM_MOST):
    n_args, n_outs = len(args), len(outs)
    far = [k for k in range(n_outs) if len(outs[k]) == 4]

    def body(*refs):
        out_refs = list(refs[n_args + len(after) :][:n_outs])
        rest = refs[n_args + len(after) + n_outs :]
        own, stages, sems = rest[: len(scratch)], rest[len(scratch) :][: len(far)], rest[len(scratch) + len(far) :]

        def copy(j, i):
            axis, pieces = outs[far[j]][2:]
            size = outs[far[j]][0][axis] // pieces
            start = i * size if isinstance(i, int) else pl.multiple_of(i * size, size)
            at = (slice(None),) * axis + (pl.ds(start, size),)
            return pltpu.make_async_copy(stages[j].at[at], out_refs[far[j]].at[at], sems[j].at[i])

        def sent(i):
            for j in range(len(far)):
                copy(j, i).start()

        shown = list(out_refs)
        for j, k in enumerate(far):
            shown[k] = stages[j]
        kernel(*refs[:n_args], *shown, *own, sent=sent)
        for j, k in enumerate(far):
            for i in range(outs[k][3]):
                copy(j, i).wait()

    near = pl.BlockSpec(memory_space=pltpu.VMEM)
    away = pl.BlockSpec(memory_space=pltpu.HBM)
    return pl.pallas_call(
        body,
        in_specs=[near] * n_args + [away] * len(after),
        out_specs=[away if k in far else near for k in range(n_outs)],
        out_shape=[jax.ShapeDtypeStruct(*o[:2]) for o in outs],
        scratch_shapes=list(scratch)
        + [pltpu.VMEM(*outs[k][:2]) for k in far]
        + [pltpu.SemaphoreType.DMA((outs[k][3],)) for k in far],
        compiler_params=pltpu.CompilerParams(vmem_limit_bytes=vmem),
        cost_estimate=pl.CostEstimate(flops=flops, bytes_accessed=4 * 2**20, transcendentals=0),
        name=name,
    )(*args, *after)


TOKEN = ((8, LANES), jnp.float32)


def transforms(parts, chans, width):
    length = parts * width
    slabs = length // LANES
    groups = chans // ROWS
    per = math.gcd(groups, 4)
    tables = make_tables(length)
    work = pltpu.VMEM((per, 2, slabs * ROWS, 2 * LANES), jnp.float32)
    outs = pltpu.VMEM((per, slabs, ROWS, LANES), jnp.float32)
    flops = 2 * 3 * 4 * groups * slabs * ROWS * 256 * 256
    pieces = groups // per
    result = ((parts, chans, width), jnp.bfloat16, 1, pieces)
    spec = ((groups, slabs * ROWS, 2 * LANES), jnp.float32, 0, pieces)

    longer = ((parts, chans + ROWS, width), jnp.bfloat16, 1, groups + 1)

    def convolve(pack, cols, after):
        args = (pack, cols, *tables)
        return place(convolve_kernel, "convolve", [result, spec, result, TOKEN], args, [work, outs], 3 * flops, after)

    def correlate(grad, spec, early):
        args = (grad, spec, early, *tables)
        return place(correlate_kernel, "correlate", [longer], args, [work, outs], 2 * flops, vmem=VMEM_ALL)[0]

    def lags(gate, grad):
        out = ((chans, length), jnp.float32, 0, pieces)
        return place(lags_kernel, "lags", [out, TOKEN], (gate, grad, *tables), [work], 3 * flops)

    def grads(back, inner, pack, gate, cols):
        tiles = pltpu.VMEM((7, chans, LANES), jnp.float32)
        out = ((8, chans), jnp.float32)
        return place(grads_kernel, "grads", [out], (back, inner, pack, gate, cols), [tiles], flops)[0]

    return convolve, correlate, lags, grads


def picks(pairs):
    rows = lax.broadcasted_iota(jnp.int32, (ROWS, LANES), 0)
    lanes = lax.broadcasted_iota(jnp.int32, (ROWS, LANES), 1)
    hit = None
    for row, lane in pairs:
        here = (rows == row) & (lanes == lane)
        hit = here if hit is None else hit | here
    return hit.astype(jnp.float32).astype(jnp.bfloat16)


def to_rows(pairs, tile):
    return lax.dot_general(picks(pairs), tile, (((1,), (1,)), ((), ())), preferred_element_type=jnp.float32)


def to_lanes(pairs, rows):
    return lax.dot_general(rows, picks(pairs), (((0,), (0,)), ((), ())), preferred_element_type=jnp.float32)


def sum_rows(row, tile_ref):
    tile = tile_ref[...]
    upper = bf16(tile)
    lower = bf16(tile - f32(upper))
    ones = bf16((lax.broadcasted_iota(jnp.int32, (ROWS, LANES), 0) == row).astype(jnp.float32))
    dot = lambda v: lax.dot_general(ones, v, (((1,), (1,)), ((), ())), preferred_element_type=jnp.float32)
    return dot(upper) + dot(lower)


def fold(value):
    tile = value[:, :LANES]
    for k in range(1, value.shape[1] // LANES):
        tile = tile + value[:, k * LANES : (k + 1) * LANES]
    return tile


def fill_earlier(fill, slot, branch, edge):
    for steps in (1, 2):
        fill[slot, steps - 1] = to_lanes([(2 * branch + 2 - steps + i, i) for i in range(steps)], edge)


def fill_later(fill, slot, branch, edge):
    for steps in (1, 2):
        fill[slot, steps - 1] = to_lanes([(2 * branch + i, LANES - steps + i) for i in range(steps)], edge)


def earlier(value, fill, slot, rows, steps):
    moved = pltpu.roll(value, steps, 1)
    lanes = lax.broadcasted_iota(jnp.int32, (value.shape[0], LANES), 1)
    first = jnp.where(lanes < steps, fill[slot, steps - 1, rows], moved[:, :LANES])
    return jnp.concatenate([first, moved[:, LANES:]], 1)


def later(value, fill, slot, rows, steps):
    count = value.shape[1]
    moved = pltpu.roll(value, count - steps, 1)
    lanes = lax.broadcasted_iota(jnp.int32, (value.shape[0], LANES), 1)
    last = jnp.where(lanes >= LANES - steps, fill[slot, steps - 1, rows], moved[:, count - LANES :])
    return jnp.concatenate([moved[:, : count - LANES], last], 1)


def over_rows(ref, body, done=None, block=32):
    piece = ref.shape[0] // PARTS
    for row in range(0, ref.shape[0], block):
        body(slice(row, row + block))
        if done and (row + block) % piece == 0:
            done(row // piece)


def edge_kernel(x0_ref, x1_ref, x2_ref, edge_ref):
    total = None
    for b, ref in enumerate((x0_ref, x1_ref, x2_ref)):
        tile = ref[:, ref.shape[1] - LANES :]
        rows = to_rows([(2 * b, LANES - 2), (2 * b + 1, LANES - 1)], tile)
        total = rows if total is None else total + rows
    edge_ref[...] = bf16(total)


def gate_kernel(x0_ref, x1_ref, x2_ref, edge_ref, cols_ref, s0_ref, s1_ref, s2_ref, gated_ref, tips_ref, fill, sent):
    edge = edge_ref[...]
    for b in range(3):
        fill_earlier(fill, b, b, edge)

    def body(rows):
        shorts = []
        for b, (x_ref, s_ref) in enumerate(((x0_ref, s0_ref), (x1_ref, s1_ref), (x2_ref, s2_ref))):
            x = f32(x_ref[rows])
            total = tap(cols_ref, rows, b, 0) * x + tap(cols_ref, rows, b, 1) * earlier(x, fill, b, rows, 1)
            shorts.append(bf16(total + tap(cols_ref, rows, b, 2) * earlier(x, fill, b, rows, 2)))
            s_ref[rows] = shorts[b]
        gated_ref[rows] = bf16(f32(shorts[1]) * f32(shorts[2]))

    over_rows(gated_ref, body, sent)
    tips = to_rows([(0, 0), (1, 1)], s2_ref[:, :LANES]) + to_rows([(2, 0), (3, 1)], s1_ref[:, :LANES])
    tips_ref[...] = bf16(tips)


def mix(rows, conv_ref, s0_ref, gated_ref, cot_ref, cols_ref):
    inner = f32(conv_ref[rows]) + column(cols_ref, rows, BIAS) * f32(gated_ref[rows])
    return inner, f32(s0_ref[rows]) * inner, f32(cot_ref[rows])


def sums_kernel(conv_ref, s0_ref, gated_ref, cot_ref, cols_ref, out_ref, sent):
    lump = lambda v: jnp.sum(v.reshape(v.shape[0] // 8, 8, v.shape[1]), 0)
    total = [jnp.zeros((8, conv_ref.shape[1]), jnp.float32)] * 2

    def body(rows):
        _, mixed, cot = mix(rows, conv_ref, s0_ref, gated_ref, cot_ref, cols_ref)
        total[0] = total[0] + lump(mixed * mixed)
        total[1] = total[1] + lump(cot * column(cols_ref, rows, GAIN) * mixed)

    over_rows(conv_ref, body)

    for k in range(2):
        out_ref[k : k + 1] = jnp.sum(total[k], 0, keepdims=True)


def norm_terms(width, part_refs):
    total = part_refs[0][...]
    for ref in part_refs[1:]:
        total = total + ref[...]
    recip = lax.rsqrt(total[0:1] / width + EPS)
    return recip, recip * recip * recip * (total[1:2] / width)


def inner_kernel(width, n_ch, *refs, sent):
    parts, (conv_ref, s0_ref, gated_ref, cot_ref, cols_ref, out_ref) = refs[:n_ch], refs[n_ch:]
    recip, cubed = norm_terms(width, parts)

    def body(rows):
        _, mixed, cot = mix(rows, conv_ref, s0_ref, gated_ref, cot_ref, cols_ref)
        d_mixed = recip * (cot * column(cols_ref, rows, GAIN)) - mixed * cubed
        out_ref[rows] = bf16(d_mixed * f32(s0_ref[rows]))

    over_rows(out_ref, body, sent)


def output_kernel(width, n_ch, *refs, sent):
    parts, refs = refs[:n_ch], refs[n_ch:]
    conv_ref, s0_ref, gated_ref, cot_ref, cols_ref, x0_ref, edge_ref, inner_ref = refs[:8]
    out_ref, g0_ref, rows_ref, after_ref, fill, tiles = refs[8:]
    recip, cubed = norm_terms(width, parts)
    fill_earlier(fill, 0, 0, edge_ref[...])

    def body(rows):
        inner, mixed, cot = mix(rows, conv_ref, s0_ref, gated_ref, cot_ref, cols_ref)
        gain = column(cols_ref, rows, GAIN)
        normed = mixed * recip
        out_ref[rows] = bf16(normed * gain)
        g0 = bf16((recip * (cot * gain) - mixed * cubed) * inner)
        g0_ref[rows] = g0
        x, g = f32(x0_ref[rows]), f32(g0)
        tiles[0, rows] = fold(g * x)
        tiles[1, rows] = fold(g * earlier(x, fill, 0, rows, 1))
        tiles[2, rows] = fold(g * earlier(x, fill, 0, rows, 2))
        tiles[3, rows] = fold(cot * normed)

    over_rows(out_ref, body, sent)
    rows_ref[...] = sum([sum_rows(k, tiles.at[k]) for k in range(4)])[:8]
    after = to_rows([(0, 0), (1, 1), (2, 0), (3, 1)], inner_ref[:, :LANES])
    after_ref[...] = bf16(after + to_rows([(4, 0), (5, 1)], g0_ref[:, :LANES]))


def adjoint(g, branch, fill, slot, rows, cols_ref):
    total = tap(cols_ref, rows, branch, 0) * g + tap(cols_ref, rows, branch, 1) * later(g, fill, slot, rows, 1)
    return bf16(total + tap(cols_ref, rows, branch, 2) * later(g, fill, slot, rows, 2))


def first_kernel(g0_ref, edge_ref, cols_ref, out_ref, token_ref, fill, sent):
    fill_later(fill, 0, 2, edge_ref[...])

    def body(rows):
        out_ref[rows] = adjoint(f32(g0_ref[rows]), 0, fill, 0, rows, cols_ref)

    over_rows(out_ref, body, sent)
    token_ref[...] = jnp.zeros_like(token_ref)


def pair_kernel(
    back_ref, inner_ref, s1_ref, s2_ref, cols_ref, tips_ref, next_ref, bias_ref, grads_ref, d1_ref, d2_ref, *refs, sent
):
    short_ref, gain_ref, fill, edge = refs
    parts, longer, _ = back_ref.shape
    own = longer - ROWS
    sums = None
    for part in range(parts):
        lanes = slice(part * own, (part + 1) * own)
        extra = f32(back_ref[part, own:, :own])
        d_gated = f32(bf16(bias_ref[:, lanes] * f32(next_ref[:, lanes]) + extra))
        edge[:, lanes] = bf16(d_gated * f32(tips_ref[:, lanes]))
        terms = extra[4:8] + extra[8:12]
        sums = terms if sums is None else sums + terms
    for k in range(2):
        fill_later(fill, k, k, edge[...])
    short_ref[0] = sums[:3]
    short_ref[1] = grads_ref[:3]
    short_ref[2] = grads_ref[3:6]
    gain_ref[...] = sums[3:4]

    def body(rows):
        part, row = rows.start // own, rows.start % own
        back = f32(back_ref[part, row : row + rows.stop - rows.start])
        d_gated = f32(bf16(column(cols_ref, rows, BIAS) * f32(inner_ref[rows]) + back))
        for b, s_ref, d_ref in ((1, s2_ref, d1_ref), (2, s1_ref, d2_ref)):
            g = f32(bf16(d_gated * f32(s_ref[rows])))
            d_ref[rows] = adjoint(g, b, fill, b - 1, rows, cols_ref)

    over_rows(d1_ref, body, sent, min(32, own))


def exchange(value):
    return lax.all_to_all(value, "ctx", split_axis=0, concat_axis=0, tiled=True)


def local(x_first, x_second, x_value, short_filter, long_filter, skip_bias, norm_gain, cotangent):
    chans, steps_dev = x_first.shape
    n_ctx = lax.axis_size("ctx")
    n_ch = lax.axis_size("ch")
    width = chans * n_ch
    own = chans // n_ctx
    convolve, correlate, lags, grads = transforms(n_ctx, own, steps_dev)
    by_dev = lambda v: v.reshape(n_ctx, own, steps_dev)
    by_pos = lambda v: v.reshape(chans, steps_dev)

    array = ((chans, steps_dev), jnp.bfloat16, 0, PARTS)
    edges = ((ROWS, chans), jnp.bfloat16)
    rows8 = ((8, chans), jnp.float32)
    fills = lambda n: pltpu.VMEM((n, 2, chans, LANES), jnp.float32)
    tiles = lambda n: pltpu.VMEM((n, chans, LANES), jnp.float32)

    pack = exchange(jnp.concatenate([by_dev(v) for v in (long_filter, x_second, x_value)], 1))
    tip = pl.BlockSpec((chans, LANES), lambda i: (0, steps_dev // LANES - 1))
    edge = pl.pallas_call(
        edge_kernel,
        grid=(1,),
        in_specs=[tip] * 3,
        out_specs=pl.BlockSpec((ROWS, chans), lambda i: (0, 0)),
        out_shape=jax.ShapeDtypeStruct(*edges),
        name="edge",
    )(x_first, x_second, x_value)
    edge = shifted(edge, "ctx", 1)
    cols = jnp.concatenate([short_filter.reshape(9, chans), skip_bias[None], norm_gain[None]], 0)
    cols = jnp.pad(cols, ((0, ROWS - 11), (0, 0))).T
    own_cols = lax.dynamic_slice_in_dim(cols, lax.axis_index("ctx") * own, own, 0)
    conv_cm, filt_spec, gated_cm, conv_done = convolve(pack, own_cols, (edge,))
    first_s, second_s, third_s, gated, tips = place(
        gate_kernel, "gate", [array] * 4 + [edges], (x_first, x_second, x_value, edge, cols), [fills(3)], after=(conv_done,), vmem=VMEM_ALL
    )
    tips = shifted(tips, "ctx", -1)
    conv = by_pos(exchange(conv_cm))
    mix_args = (conv, first_s, gated, cotangent, cols)
    sums = place(sums_kernel, "sums", [((2, steps_dev), jnp.float32)], mix_args)[0]
    parts = [sums]
    for k in range(1, n_ch):
        parts.append(lax.ppermute(sums, "ch", [(i, i ^ k) for i in range(n_ch)]))
    inner_part = lambda *refs, sent: inner_kernel(width, n_ch, *refs, sent=sent)
    d_inner = place(inner_part, "inner", [array], (*parts, *mix_args))[0]
    d_inner_cm = exchange(by_dev(d_inner))
    output, grad_first, early_rows, after = place(
        lambda *refs, sent: output_kernel(width, n_ch, *refs, sent=sent),
        "output",
        [array, array, rows8, edges],
        (*parts, *mix_args, x_first, edge, d_inner),
        [fills(1), tiles(4)],
    )
    after = shifted(after, "ctx", -1)
    back_cm = correlate(d_inner_cm, filt_spec, early_rows)
    back = exchange(back_cm)
    d_first, first_done = place(first_kernel, "first", [array, TOKEN], (grad_first, after, cols), [fills(1)])
    own_rows = grads(back_cm, d_inner_cm, pack, gated_cm, own_cols)
    d_long, lags_done = lags(gated_cm, d_inner_cm)
    d_second, d_value, d_short, d_gain = place(
        pair_kernel,
        "pair",
        [array, array, ((3, 3, own), jnp.float32), ((1, own), jnp.float32)],
        (back, d_inner, second_s, third_s, cols, tips, after, skip_bias[None], own_rows),
        [fills(2), pltpu.VMEM(*edges)],
        after=(first_done, lags_done),
    )
    return (output, d_first, d_second, d_value, d_long, d_short, own_rows[6], d_gain[0])


def solution(mesh):
    seq = P("ch", "ctx")
    own = ("ch", "ctx")
    return jax.shard_map(
        local,
        mesh=mesh,
        in_specs=(seq, seq, seq, P(None, None, "ch"), seq, P("ch"), P("ch"), seq),
        out_specs=(seq, seq, seq, seq, P(own, None), P(None, None, own), P(own), P(own)),
        check_vma=False,
    )
```

```python
import math

import jax
import jax.numpy as jnp
import numpy as np
from jax import lax
from jax.experimental import pallas as pl
from jax.experimental.pallas import tpu as pltpu
from jax.sharding import PartitionSpec as P

EPS = 1e-06
LANES = 128
ROWS = 16
HALF = 8
VMEM_MOST = 24 * 2**20
VMEM_ALL = 60 * 2**20
VMEM_FFT = 50 * 2**20
PARTS = 4


def f32(value):
    return value.astype(jnp.float32)


def bf16(value):
    return value.astype(jnp.bfloat16)


def shifted(value, axis, steps):
    count = lax.axis_size(axis)
    first, last = (max(0, -steps), min(count, count - steps))
    return lax.ppermute(value, axis, [(source, source + steps) for source in range(first, last)])


def root(angle):
    return math.cos(2 * math.pi * angle), math.sin(2 * math.pi * angle)


def slab_angles(slabs):
    angles = [-0.25]
    while len(angles) < slabs:
        angles = [a / 2 + extra for a in angles for extra in (0.0, 0.5)]
    return angles


def split_angles(slabs):
    levels, angles = [], [-0.25]
    while len(angles) < slabs:
        levels.append([a / 2 for a in angles])
        angles = [a / 2 + extra for a in angles for extra in (0.0, 0.5)]
    return levels


def slabs_forward(xs):
    slabs = len(xs)
    data = None
    for level, turns in enumerate(split_angles(slabs)):
        size = slabs >> level
        half = size // 2
        new = [None] * slabs
        for b, turn in enumerate(turns):
            c, s = root(turn)
            for n in range(half):
                lo, hi = b * size + n, b * size + n + half
                if data is None:
                    tr, ti = xs[hi] * c, xs[hi] * s
                    new[lo] = (xs[lo] + tr, ti)
                    new[hi] = (xs[lo] - tr, -ti)
                else:
                    (ar, ai), (br, bi) = data[lo], data[hi]
                    tr, ti = br * c - bi * s, br * s + bi * c
                    new[lo] = (ar + tr, ai + ti)
                    new[hi] = (ar - tr, ai - ti)
        data = new
    return data


def slabs_inverse(data):
    slabs = len(data)
    levels = split_angles(slabs)
    for level in range(len(levels) - 1, -1, -1):
        size = slabs >> level
        half = size // 2
        new = [None] * slabs
        for b, turn in enumerate(levels[level]):
            c, s = root(turn)
            for n in range(half):
                lo, hi = b * size + n, b * size + n + half
                (ur, ui), (vr, vi) = data[lo], data[hi]
                dr, di = ur - vr, ui - vi
                if level == 0:
                    new[lo] = ur + vr
                    new[hi] = dr * c + di * s
                else:
                    new[lo] = (ur + vr, ui + vi)
                    new[hi] = (dr * c + di * s, di * c - dr * s)
        data = new
    return data


def make_tables(length):
    slabs = length // LANES
    angle = np.array(slab_angles(slabs))[:, None] * np.arange(LANES)[None, :] / LANES
    twist = np.stack([np.cos(2 * np.pi * angle), np.sin(2 * np.pi * angle)], 1).astype(np.float32)
    grid = np.arange(LANES)[:, None] * np.arange(LANES)[None, :] % LANES * (2 * np.pi / LANES)
    cos, sin = np.cos(grid), np.sin(grid)
    fwd = np.block([[cos, -sin], [sin, cos]]).astype(np.float32)
    inv = np.block([[cos, sin], [-sin, cos]]).astype(np.float32)

    def two(mat):
        upper = mat.astype(jnp.bfloat16)
        lower = (mat - upper.astype(np.float32)).astype(jnp.bfloat16)
        return np.stack([upper, lower])

    return jnp.asarray(np.stack([twist, twist / length])), jnp.asarray(two(fwd)), jnp.asarray(two(inv))


def split_dot(value, mat_ref):
    upper = value.astype(jnp.bfloat16)
    lower = (value - upper.astype(jnp.float32)).astype(jnp.bfloat16)
    dot = lambda a, b: jnp.dot(a, b, preferred_element_type=jnp.float32)
    return dot(upper, mat_ref[0]) + (dot(lower, mat_ref[0]) + dot(upper, mat_ref[1]))


def forward_group(x_ref, row, twist_ref, mat_ref, work):
    parts, _, width = x_ref.shape
    per = width // LANES
    slabs = parts * per
    xs = [f32(x_ref[s // per, pl.ds(row, ROWS), s % per * LANES : (s % per + 1) * LANES]) for s in range(slabs)]
    for h in range(0, ROWS, HALF):
        data = slabs_forward([x[h : h + HALF] for x in xs])
        for j, (re, im) in enumerate(data):
            tc, ts = twist_ref[j, 0:1], twist_ref[j, 1:2]
            work[j * ROWS + h : j * ROWS + h + HALF, :LANES] = re * tc - im * ts
            work[j * ROWS + h : j * ROWS + h + HALF, LANES:] = re * ts + im * tc
    return split_dot(work[...], mat_ref)


def inverse_group(spec, twist_ref, mat_ref, work, store):
    slabs = spec.shape[0] // ROWS
    work[...] = split_dot(spec, mat_ref)
    for h in range(0, ROWS, HALF):
        data = []
        for j in range(slabs):
            tc, ts = twist_ref[j, 0:1], twist_ref[j, 1:2]
            re = work[j * ROWS + h : j * ROWS + h + HALF, :LANES]
            im = work[j * ROWS + h : j * ROWS + h + HALF, LANES:]
            data.append((re * tc + im * ts, im * tc - re * ts))
        for s, value in enumerate(slabs_inverse(data)):
            store(s, h, value)


def product(a, b):
    ar, ai, br, bi = a[:, :LANES], a[:, LANES:], b[:, :LANES], b[:, LANES:]
    return jnp.concatenate([ar * br - ai * bi, ar * bi + ai * br], 1)


def conj_product(a, b):
    ar, ai, br, bi = a[:, :LANES], a[:, LANES:], b[:, :LANES], b[:, LANES:]
    return jnp.concatenate([ar * br + ai * bi, ar * bi - ai * br], 1)


def spectrum_pair(filt_ref, gate_ref, row, twist_ref, fwd_ref, work):
    one = forward_group(filt_ref, row, twist_ref.at[0], fwd_ref, work.at[0])
    return one, forward_group(gate_ref, row, twist_ref.at[0], fwd_ref, work.at[1])


def put_slabs(out_ref, row, slabs_ref):
    per = out_ref.shape[2] // LANES
    for s in range(slabs_ref.shape[0]):
        lanes = slice(s % per * LANES, (s % per + 1) * LANES)
        out_ref[s // per, pl.ds(row, ROWS), lanes] = bf16(slabs_ref[s])


def storing(slabs_ref):
    def store(s, h, value):
        slabs_ref[s, h : h + HALF] = value

    return store


def over_groups(count, per, body, done):
    def step(i, carry):
        for g in range(per):
            body(g, pl.multiple_of((i * per + g) * ROWS, ROWS))
        done(i)
        return carry

    lax.fori_loop(0, count // per, step, 0)


def column(cols_ref, rows, k):
    return cols_ref[rows, k : k + 1]


def tap(cols_ref, rows, branch, k):
    return column(cols_ref, rows, 3 * branch + k)


BIAS, GAIN = 9, 10


def after_wrap(now, before, steps):
    lanes = lax.broadcasted_iota(jnp.int32, now.shape, 1)
    return jnp.where(lanes < steps, before, now)


def short_slabs(x_ref, row, taps):
    parts, _, width = x_ref.shape
    per = width // LANES
    result, last = [], [0.0, 0.0]
    for s in range(parts * per):
        x = f32(x_ref[s // per, pl.ds(row, ROWS), s % per * LANES : (s % per + 1) * LANES])
        moved = [pltpu.roll(x, k, 1) for k in (1, 2)]
        one, two = (after_wrap(moved[k], last[k], k + 1) for k in range(2))
        result.append(bf16(taps[0] * x + taps[1] * one + taps[2] * two))
        last = moved
    return result


def convolve_kernel(pack_ref, cols_ref, twist_ref, fwd_ref, inv_ref, out_ref, spec_ref, gate_ref, token_ref, work, slabs, sent):
    chans = out_ref.shape[1]
    per = out_ref.shape[2] // LANES
    filt_ref, x1_ref, x2_ref = (pack_ref.at[:, k * chans : (k + 1) * chans] for k in range(3))

    def body(g, row):
        rows = pl.ds(row, ROWS)
        s1, s2 = (
            short_slabs(ref, row, [tap(cols_ref, rows, b, k) for k in range(3)]) for b, ref in ((1, x1_ref), (2, x2_ref))
        )
        for s, (one, two) in enumerate(zip(s1, s2)):
            gate_ref[s // per, rows, s % per * LANES : (s % per + 1) * LANES] = bf16(f32(one) * f32(two))
        filt, gate = spectrum_pair(filt_ref, gate_ref, row, twist_ref, fwd_ref, work.at[g])
        spec_ref[row // ROWS] = filt
        inverse_group(product(filt, gate), twist_ref.at[1], inv_ref, work.at[g, 0], storing(slabs.at[g]))
        put_slabs(out_ref, row, slabs.at[g])

    over_groups(chans // ROWS, work.shape[0], body, sent)
    token_ref[...] = jnp.zeros_like(token_ref)


def correlate_kernel(grad_ref, spec_ref, early_ref, twist_ref, fwd_ref, inv_ref, out_ref, work, slabs, sent):
    parts, chans, width = grad_ref.shape
    groups, per = chans // ROWS, work.shape[0]

    def body(g, row):
        grad = forward_group(grad_ref, row, twist_ref.at[0], fwd_ref, work.at[g, 0])
        mixed = conj_product(spec_ref[row // ROWS], grad)
        inverse_group(mixed, twist_ref.at[1], inv_ref, work.at[g, 0], storing(slabs.at[g]))
        put_slabs(out_ref, row, slabs.at[g])

    def done(i):
        for g in range(per):
            sent(i * per + g)

    over_groups(groups, per, body, done)
    for part in range(parts):
        sums = early_ref[:4, part * chans : (part + 1) * chans]
        upper = f32(bf16(sums))
        if part + 1 < parts:
            tips = to_rows([(0, 0), (1, 1), (2, 0), (3, 1)], out_ref[part + 1, :chans, :LANES])[:4]
        else:
            tips = jnp.zeros((4, chans), jnp.float32)
        rows = jnp.concatenate([tips, upper, sums - upper, jnp.zeros((4, chans), jnp.float32)], 0)
        rows = jnp.concatenate([rows, jnp.zeros((ROWS, width - chans), jnp.float32)], 1)
        out_ref[part, chans:] = bf16(rows)
    sent(groups)


def grads_kernel(back_ref, inner_ref, pack_ref, gate_ref, cols_ref, rows_ref, tiles, sent):
    parts, chans, _ = inner_ref.shape
    block = min(32, chans)
    for row in range(0, chans, block):
        rows = slice(row, row + block)
        taps = [[tap(cols_ref, rows, b, k) for k in range(3)] for b in range(3)]
        bias = column(cols_ref, rows, BIAS)
        totals, last = [None] * 7, [[None] * 2, [None] * 2]
        for part in range(parts):
            moved, shorts = [], []
            for b in (1, 2):
                x = f32(pack_ref[part, b * chans + row : b * chans + row + block])
                turns = [pltpu.roll(x, k, 1) for k in (1, 2)]
                fixed = []
                for k in range(2):
                    before = 0.0 if part == 0 else last[b - 1][k]
                    head = after_wrap(turns[k][:, :LANES], before, k + 1)
                    fixed.append(jnp.concatenate([head, turns[k][:, LANES:]], 1))
                    last[b - 1][k] = turns[k][:, :LANES]
                moved.append([x] + fixed)
                shorts.append(f32(bf16(taps[b][0] * x + taps[b][1] * fixed[0] + taps[b][2] * fixed[1])))
            inner = f32(inner_ref[part, rows])
            d_gated = f32(bf16(bias * inner + f32(back_ref[part, rows])))
            terms = []
            for b in (1, 2):
                g = f32(bf16(d_gated * shorts[2 - b]))
                terms += [fold(g * moved[b - 1][k]) for k in range(3)]
            terms.append(fold(inner * f32(gate_ref[part, rows])))
            totals = [t if total is None else total + t for total, t in zip(totals, terms)]
        for k in range(7):
            tiles[k, rows] = totals[k]
    rows_ref[...] = sum([sum_rows(k, tiles.at[k]) for k in range(7)])[:8]


def lags_kernel(gate_ref, grad_ref, twist_ref, fwd_ref, inv_ref, out_ref, token_ref, work, sent):
    chans = out_ref.shape[0]
    def body(g, row):
        def store(s, h, value):
            out_ref[pl.ds(pl.multiple_of(row + h, HALF), HALF), s * LANES : (s + 1) * LANES] = value

        gate, grad = spectrum_pair(gate_ref, grad_ref, row, twist_ref, fwd_ref, work.at[g])
        inverse_group(conj_product(gate, grad), twist_ref.at[1], inv_ref, work.at[g, 0], store)

    over_groups(chans // ROWS, work.shape[0], body, sent)
    token_ref[...] = jnp.zeros_like(token_ref)


def place(kernel, name, outs, args, scratch=(), flops=10**6, after=(), vmem=VMEM_MOST, lazy=()):
    n_args, n_outs = len(args), len(outs)
    drawn = [a[0] for a in lazy]
    far = [k for k in range(n_outs) if len(outs[k]) == 4]

    def body(*refs):
        out_refs = list(refs[n_args + len(after) :][:n_outs])
        rest = refs[n_args + len(after) + n_outs :]
        own, rest = rest[: len(scratch)], rest[len(scratch) :]
        stages, rest = rest[: len(far)], rest[len(far) :]
        sems, rest = rest[: len(far)], rest[len(far) :]
        held, waits = rest[: len(lazy)], rest[len(lazy) :]
        ins = list(refs[:n_args])

        def fetch(j, i):
            k, axis, pieces = lazy[j]
            size = args[k].shape[axis] // pieces
            start = i * size if isinstance(i, int) else pl.multiple_of(i * size, size)
            at = (slice(None),) * axis + (pl.ds(start, size),)
            return pltpu.make_async_copy(refs[k].at[at], held[j].at[at], waits[j].at[i])

        for i in range(max([a[2] for a in lazy], default=0)):
            for j in range(len(lazy)):
                if i < lazy[j][2]:
                    fetch(j, i).start()
        for j, k in enumerate(drawn):
            ins[k] = held[j]

        def need(i=None):
            for j in range(len(lazy)):
                if (i is None) == (lazy[j][2] == 1):
                    fetch(j, 0 if i is None else i).wait()


        def copy(j, i):
            axis, pieces = outs[far[j]][2:]
            size = outs[far[j]][0][axis] // pieces
            start = i * size if isinstance(i, int) else pl.multiple_of(i * size, size)
            at = (slice(None),) * axis + (pl.ds(start, size),)
            return pltpu.make_async_copy(stages[j].at[at], out_refs[far[j]].at[at], sems[j].at[i])

        def sent(i):
            for j in range(len(far)):
                copy(j, i).start()

        shown = list(out_refs)
        for j, k in enumerate(far):
            shown[k] = stages[j]
        more = {"need": need} if lazy else {}
        kernel(*ins, *shown, *own, sent=sent, **more)
        for j, k in enumerate(far):
            for i in range(outs[k][3]):
                copy(j, i).wait()

    near = pl.BlockSpec(memory_space=pltpu.VMEM)
    away = pl.BlockSpec(memory_space=pltpu.HBM)
    return pl.pallas_call(
        body,
        in_specs=[away if k in drawn else near for k in range(n_args)] + [away] * len(after),
        out_specs=[away if k in far else near for k in range(n_outs)],
        out_shape=[jax.ShapeDtypeStruct(*o[:2]) for o in outs],
        scratch_shapes=list(scratch)
        + [pltpu.VMEM(*outs[k][:2]) for k in far]
        + [pltpu.SemaphoreType.DMA((outs[k][3],)) for k in far]
        + [pltpu.VMEM(args[k].shape, args[k].dtype) for k in drawn]
        + [pltpu.SemaphoreType.DMA((a[2],)) for a in lazy],
        compiler_params=pltpu.CompilerParams(vmem_limit_bytes=vmem),
        cost_estimate=pl.CostEstimate(flops=flops, bytes_accessed=4 * 2**20, transcendentals=0),
        name=name,
    )(*args, *after)


TOKEN = ((8, LANES), jnp.float32)


def transforms(parts, chans, width):
    length = parts * width
    slabs = length // LANES
    groups = chans // ROWS
    per = math.gcd(groups, 4)
    tables = make_tables(length)
    work = pltpu.VMEM((per, 2, slabs * ROWS, 2 * LANES), jnp.float32)
    outs = pltpu.VMEM((per, slabs, ROWS, LANES), jnp.float32)
    flops = 2 * 3 * 4 * groups * slabs * ROWS * 256 * 256
    pieces = groups // per
    result = ((parts, chans, width), jnp.bfloat16, 1, pieces)
    spec = ((groups, slabs * ROWS, 2 * LANES), jnp.float32, 0, pieces)

    longer = ((parts, chans + ROWS, width), jnp.bfloat16, 1, groups + 1)

    def convolve(pack, cols, after):
        args = (pack, cols, *tables)
        return place(convolve_kernel, "convolve", [result, spec, result, TOKEN], args, [work, outs], 3 * flops, after, VMEM_FFT)

    def correlate(grad, spec, early):
        args = (grad, spec, early, *tables)
        return place(correlate_kernel, "correlate", [longer], args, [work, outs], 2 * flops, vmem=VMEM_ALL)[0]

    def lags(gate, grad):
        out = ((chans, length), jnp.float32, 0, pieces)
        return place(lags_kernel, "lags", [out, TOKEN], (gate, grad, *tables), [work], 3 * flops)

    def grads(back, inner, pack, gate, cols):
        tiles = pltpu.VMEM((7, chans, LANES), jnp.float32)
        out = ((8, chans), jnp.float32)
        return place(grads_kernel, "grads", [out], (back, inner, pack, gate, cols), [tiles], flops)[0]

    return convolve, correlate, lags, grads


def picks(pairs):
    rows = lax.broadcasted_iota(jnp.int32, (ROWS, LANES), 0)
    lanes = lax.broadcasted_iota(jnp.int32, (ROWS, LANES), 1)
    hit = None
    for row, lane in pairs:
        here = (rows == row) & (lanes == lane)
        hit = here if hit is None else hit | here
    return hit.astype(jnp.float32).astype(jnp.bfloat16)


def to_rows(pairs, tile):
    return lax.dot_general(picks(pairs), tile, (((1,), (1,)), ((), ())), preferred_element_type=jnp.float32)


def to_lanes(pairs, rows):
    return lax.dot_general(rows, picks(pairs), (((0,), (0,)), ((), ())), preferred_element_type=jnp.float32)


def sum_rows(row, tile_ref):
    tile = tile_ref[...]
    upper = bf16(tile)
    lower = bf16(tile - f32(upper))
    ones = bf16((lax.broadcasted_iota(jnp.int32, (ROWS, LANES), 0) == row).astype(jnp.float32))
    dot = lambda v: lax.dot_general(ones, v, (((1,), (1,)), ((), ())), preferred_element_type=jnp.float32)
    return dot(upper) + dot(lower)


def fold(value):
    tile = value[:, :LANES]
    for k in range(1, value.shape[1] // LANES):
        tile = tile + value[:, k * LANES : (k + 1) * LANES]
    return tile


def fill_earlier(fill, slot, branch, edge):
    for steps in (1, 2):
        fill[slot, steps - 1] = to_lanes([(2 * branch + 2 - steps + i, i) for i in range(steps)], edge)


def fill_later(fill, slot, branch, edge):
    for steps in (1, 2):
        fill[slot, steps - 1] = to_lanes([(2 * branch + i, LANES - steps + i) for i in range(steps)], edge)


def earlier(value, fill, slot, rows, steps):
    moved = pltpu.roll(value, steps, 1)
    lanes = lax.broadcasted_iota(jnp.int32, (value.shape[0], LANES), 1)
    first = jnp.where(lanes < steps, fill[slot, steps - 1, rows], moved[:, :LANES])
    return jnp.concatenate([first, moved[:, LANES:]], 1)


def later(value, fill, slot, rows, steps):
    count = value.shape[1]
    moved = pltpu.roll(value, count - steps, 1)
    lanes = lax.broadcasted_iota(jnp.int32, (value.shape[0], LANES), 1)
    last = jnp.where(lanes >= LANES - steps, fill[slot, steps - 1, rows], moved[:, count - LANES :])
    return jnp.concatenate([moved[:, : count - LANES], last], 1)


def over_rows(ref, body, done=None, block=32, before=None):
    piece = ref.shape[0] // PARTS
    for row in range(0, ref.shape[0], block):
        if before and row % piece == 0:
            before(row // piece)
        body(slice(row, row + block))
        if done and (row + block) % piece == 0:
            done(row // piece)


def edge_kernel(x0_ref, x1_ref, x2_ref, edge_ref):
    total = None
    for b, ref in enumerate((x0_ref, x1_ref, x2_ref)):
        tile = ref[:, ref.shape[1] - LANES :]
        rows = to_rows([(2 * b, LANES - 2), (2 * b + 1, LANES - 1)], tile)
        total = rows if total is None else total + rows
    edge_ref[...] = bf16(total)


def gate_kernel(x0_ref, x1_ref, x2_ref, edge_ref, cols_ref, s0_ref, s1_ref, s2_ref, gated_ref, tips_ref, fill, sent):
    edge = edge_ref[...]
    for b in range(3):
        fill_earlier(fill, b, b, edge)

    def body(rows):
        shorts = []
        for b, (x_ref, s_ref) in enumerate(((x0_ref, s0_ref), (x1_ref, s1_ref), (x2_ref, s2_ref))):
            x = f32(x_ref[rows])
            total = tap(cols_ref, rows, b, 0) * x + tap(cols_ref, rows, b, 1) * earlier(x, fill, b, rows, 1)
            shorts.append(bf16(total + tap(cols_ref, rows, b, 2) * earlier(x, fill, b, rows, 2)))
            s_ref[rows] = shorts[b]
        gated_ref[rows] = bf16(f32(shorts[1]) * f32(shorts[2]))

    over_rows(gated_ref, body, sent)
    tips = to_rows([(0, 0), (1, 1)], s2_ref[:, :LANES]) + to_rows([(2, 0), (3, 1)], s1_ref[:, :LANES])
    tips_ref[...] = bf16(tips)


def mix(rows, conv_ref, s0_ref, gated_ref, cot_ref, cols_ref):
    inner = f32(conv_ref[rows]) + column(cols_ref, rows, BIAS) * f32(gated_ref[rows])
    return inner, f32(s0_ref[rows]) * inner, f32(cot_ref[rows])


def sums_kernel(conv_ref, s0_ref, gated_ref, cot_ref, cols_ref, out_ref, sent):
    lump = lambda v: jnp.sum(v.reshape(v.shape[0] // 8, 8, v.shape[1]), 0)
    total = [jnp.zeros((8, conv_ref.shape[1]), jnp.float32)] * 2

    def body(rows):
        _, mixed, cot = mix(rows, conv_ref, s0_ref, gated_ref, cot_ref, cols_ref)
        total[0] = total[0] + lump(mixed * mixed)
        total[1] = total[1] + lump(cot * column(cols_ref, rows, GAIN) * mixed)

    over_rows(conv_ref, body)

    for k in range(2):
        out_ref[k : k + 1] = jnp.sum(total[k], 0, keepdims=True)


def norm_terms(width, part_refs):
    total = part_refs[0][...]
    for ref in part_refs[1:]:
        total = total + ref[...]
    recip = lax.rsqrt(total[0:1] / width + EPS)
    return recip, recip * recip * recip * (total[1:2] / width)


def inner_kernel(width, n_ch, *refs, sent):
    parts, (conv_ref, s0_ref, gated_ref, cot_ref, cols_ref, out_ref) = refs[:n_ch], refs[n_ch:]
    recip, cubed = norm_terms(width, parts)

    def body(rows):
        _, mixed, cot = mix(rows, conv_ref, s0_ref, gated_ref, cot_ref, cols_ref)
        d_mixed = recip * (cot * column(cols_ref, rows, GAIN)) - mixed * cubed
        out_ref[rows] = bf16(d_mixed * f32(s0_ref[rows]))

    over_rows(out_ref, body, sent)


def output_kernel(width, n_ch, *refs, sent):
    parts, refs = refs[:n_ch], refs[n_ch:]
    conv_ref, s0_ref, gated_ref, cot_ref, cols_ref, x0_ref, edge_ref, inner_ref = refs[:8]
    out_ref, g0_ref, rows_ref, after_ref, fill, tiles = refs[8:]
    recip, cubed = norm_terms(width, parts)
    fill_earlier(fill, 0, 0, edge_ref[...])

    def body(rows):
        inner, mixed, cot = mix(rows, conv_ref, s0_ref, gated_ref, cot_ref, cols_ref)
        gain = column(cols_ref, rows, GAIN)
        normed = mixed * recip
        out_ref[rows] = bf16(normed * gain)
        g0 = bf16((recip * (cot * gain) - mixed * cubed) * inner)
        g0_ref[rows] = g0
        x, g = f32(x0_ref[rows]), f32(g0)
        tiles[0, rows] = fold(g * x)
        tiles[1, rows] = fold(g * earlier(x, fill, 0, rows, 1))
        tiles[2, rows] = fold(g * earlier(x, fill, 0, rows, 2))
        tiles[3, rows] = fold(cot * normed)

    over_rows(out_ref, body, sent)
    rows_ref[...] = sum([sum_rows(k, tiles.at[k]) for k in range(4)])[:8]
    after = to_rows([(0, 0), (1, 1), (2, 0), (3, 1)], inner_ref[:, :LANES])
    after_ref[...] = bf16(after + to_rows([(4, 0), (5, 1)], g0_ref[:, :LANES]))


def adjoint(g, branch, fill, slot, rows, cols_ref):
    total = tap(cols_ref, rows, branch, 0) * g + tap(cols_ref, rows, branch, 1) * later(g, fill, slot, rows, 1)
    return bf16(total + tap(cols_ref, rows, branch, 2) * later(g, fill, slot, rows, 2))


def first_kernel(g0_ref, edge_ref, cols_ref, out_ref, token_ref, fill, sent):
    fill_later(fill, 0, 2, edge_ref[...])

    def body(rows):
        out_ref[rows] = adjoint(f32(g0_ref[rows]), 0, fill, 0, rows, cols_ref)

    over_rows(out_ref, body, sent)
    token_ref[...] = jnp.zeros_like(token_ref)


def pair_kernel(
    back_ref, inner_ref, s1_ref, s2_ref, cols_ref, tips_ref, next_ref, bias_ref, grads_ref, d1_ref, d2_ref, *refs, sent, need
):
    short_ref, gain_ref, fill, edge = refs
    parts, longer, _ = back_ref.shape
    own = longer - ROWS
    sums = None
    for part in range(parts):
        lanes = slice(part * own, (part + 1) * own)
        extra = f32(back_ref[part, own:, :own])
        d_gated = f32(bf16(bias_ref[:, lanes] * f32(next_ref[:, lanes]) + extra))
        edge[:, lanes] = bf16(d_gated * f32(tips_ref[:, lanes]))
        terms = extra[4:8] + extra[8:12]
        sums = terms if sums is None else sums + terms
    for k in range(2):
        fill_later(fill, k, k, edge[...])
    short_ref[0] = sums[:3]
    short_ref[1] = grads_ref[:3]
    short_ref[2] = grads_ref[3:6]
    gain_ref[...] = sums[3:4]

    def body(rows):
        part, row = rows.start // own, rows.start % own
        back = f32(back_ref[part, row : row + rows.stop - rows.start])
        d_gated = f32(bf16(column(cols_ref, rows, BIAS) * f32(inner_ref[rows]) + back))
        for b, s_ref, d_ref in ((1, s2_ref, d1_ref), (2, s1_ref, d2_ref)):
            g = f32(bf16(d_gated * f32(s_ref[rows])))
            d_ref[rows] = adjoint(g, b, fill, b - 1, rows, cols_ref)

    over_rows(d1_ref, body, sent, min(32, own), need)


def exchange(value):
    return lax.all_to_all(value, "ctx", split_axis=0, concat_axis=0, tiled=True)


def local(x_first, x_second, x_value, short_filter, long_filter, skip_bias, norm_gain, cotangent):
    chans, steps_dev = x_first.shape
    n_ctx = lax.axis_size("ctx")
    n_ch = lax.axis_size("ch")
    width = chans * n_ch
    own = chans // n_ctx
    convolve, correlate, lags, grads = transforms(n_ctx, own, steps_dev)
    by_dev = lambda v: v.reshape(n_ctx, own, steps_dev)
    by_pos = lambda v: v.reshape(chans, steps_dev)

    array = ((chans, steps_dev), jnp.bfloat16, 0, PARTS)
    edges = ((ROWS, chans), jnp.bfloat16)
    rows8 = ((8, chans), jnp.float32)
    fills = lambda n: pltpu.VMEM((n, 2, chans, LANES), jnp.float32)
    tiles = lambda n: pltpu.VMEM((n, chans, LANES), jnp.float32)

    pack = exchange(jnp.concatenate([by_dev(v) for v in (long_filter, x_second, x_value)], 1))
    tip = pl.BlockSpec((chans, LANES), lambda i: (0, steps_dev // LANES - 1))
    edge = pl.pallas_call(
        edge_kernel,
        grid=(1,),
        in_specs=[tip] * 3,
        out_specs=pl.BlockSpec((ROWS, chans), lambda i: (0, 0)),
        out_shape=jax.ShapeDtypeStruct(*edges),
        name="edge",
    )(x_first, x_second, x_value)
    edge = shifted(edge, "ctx", 1)
    cols = jnp.concatenate([short_filter.reshape(9, chans), skip_bias[None], norm_gain[None]], 0)
    cols = jnp.pad(cols, ((0, ROWS - 11), (0, 0))).T
    own_cols = lax.dynamic_slice_in_dim(cols, lax.axis_index("ctx") * own, own, 0)
    conv_cm, filt_spec, gated_cm, conv_done = convolve(pack, own_cols, (edge,))
    first_s, second_s, third_s, gated, tips = place(
        gate_kernel, "gate", [array] * 4 + [edges], (x_first, x_second, x_value, edge, cols), [fills(3)], after=(conv_done,), vmem=VMEM_ALL
    )
    tips = shifted(tips, "ctx", -1)
    conv = by_pos(exchange(conv_cm))
    mix_args = (conv, first_s, gated, cotangent, cols)
    sums = place(sums_kernel, "sums", [((2, steps_dev), jnp.float32)], mix_args)[0]
    parts = [sums]
    for k in range(1, n_ch):
        parts.append(lax.ppermute(sums, "ch", [(i, i ^ k) for i in range(n_ch)]))
    inner_part = lambda *refs, sent: inner_kernel(width, n_ch, *refs, sent=sent)
    d_inner = place(inner_part, "inner", [array], (*parts, *mix_args))[0]
    d_inner_cm = exchange(by_dev(d_inner))
    output, grad_first, early_rows, after = place(
        lambda *refs, sent: output_kernel(width, n_ch, *refs, sent=sent),
        "output",
        [array, array, rows8, edges],
        (*parts, *mix_args, x_first, edge, d_inner),
        [fills(1), tiles(4)],
    )
    after = shifted(after, "ctx", -1)
    back_cm = correlate(d_inner_cm, filt_spec, early_rows)
    back = exchange(back_cm)
    d_first, first_done = place(first_kernel, "first", [array, TOKEN], (grad_first, after, cols), [fills(1)])
    own_rows = grads(back_cm, d_inner_cm, pack, gated_cm, own_cols)
    d_long, lags_done = lags(gated_cm, d_inner_cm)
    d_second, d_value, d_short, d_gain = place(
        pair_kernel,
        "pair",
        [array, array, ((3, 3, own), jnp.float32), ((1, own), jnp.float32)],
        (back, d_inner, second_s, third_s, cols, tips, after, skip_bias[None], own_rows),
        [fills(2), pltpu.VMEM(*edges)],
        after=(first_done, lags_done),
        lazy=[(1, 0, PARTS)],
    )
    return (output, d_first, d_second, d_value, d_long, d_short, own_rows[6], d_gain[0])


def solution(mesh):
    seq = P("ch", "ctx")
    own = ("ch", "ctx")
    return jax.shard_map(
        local,
        mesh=mesh,
        in_specs=(seq, seq, seq, P(None, None, "ch"), seq, P("ch"), P("ch"), seq),
        out_specs=(seq, seq, seq, seq, P(own, None), P(None, None, own), P(own), P(own)),
        check_vma=False,
    )
```

```python
import math

import jax
import jax.numpy as jnp
import numpy as np
from jax import lax
from jax.experimental import pallas as pl
from jax.experimental.pallas import tpu as pltpu
from jax.sharding import PartitionSpec as P

EPS = 1e-06
LANES = 128
ROWS = 16
HALF = 8
VMEM_MOST = 24 * 2**20
VMEM_ALL = 60 * 2**20
VMEM_FFT = 50 * 2**20
PARTS = 4


def f32(value):
    return value.astype(jnp.float32)


def bf16(value):
    return value.astype(jnp.bfloat16)


def shifted(value, axis, steps):
    count = lax.axis_size(axis)
    first, last = (max(0, -steps), min(count, count - steps))
    return lax.ppermute(value, axis, [(source, source + steps) for source in range(first, last)])


def root(angle):
    return math.cos(2 * math.pi * angle), math.sin(2 * math.pi * angle)


def slab_angles(slabs):
    angles = [-0.25]
    while len(angles) < slabs:
        angles = [a / 2 + extra for a in angles for extra in (0.0, 0.5)]
    return angles


def split_angles(slabs):
    levels, angles = [], [-0.25]
    while len(angles) < slabs:
        levels.append([a / 2 for a in angles])
        angles = [a / 2 + extra for a in angles for extra in (0.0, 0.5)]
    return levels


def slabs_forward(xs):
    slabs = len(xs)
    data = None
    for level, turns in enumerate(split_angles(slabs)):
        size = slabs >> level
        half = size // 2
        new = [None] * slabs
        for b, turn in enumerate(turns):
            c, s = root(turn)
            for n in range(half):
                lo, hi = b * size + n, b * size + n + half
                if data is None:
                    tr, ti = xs[hi] * c, xs[hi] * s
                    new[lo] = (xs[lo] + tr, ti)
                    new[hi] = (xs[lo] - tr, -ti)
                else:
                    (ar, ai), (br, bi) = data[lo], data[hi]
                    tr, ti = br * c - bi * s, br * s + bi * c
                    new[lo] = (ar + tr, ai + ti)
                    new[hi] = (ar - tr, ai - ti)
        data = new
    return data


def slabs_inverse(data):
    slabs = len(data)
    levels = split_angles(slabs)
    for level in range(len(levels) - 1, -1, -1):
        size = slabs >> level
        half = size // 2
        new = [None] * slabs
        for b, turn in enumerate(levels[level]):
            c, s = root(turn)
            for n in range(half):
                lo, hi = b * size + n, b * size + n + half
                (ur, ui), (vr, vi) = data[lo], data[hi]
                dr, di = ur - vr, ui - vi
                if level == 0:
                    new[lo] = ur + vr
                    new[hi] = dr * c + di * s
                else:
                    new[lo] = (ur + vr, ui + vi)
                    new[hi] = (dr * c + di * s, di * c - dr * s)
        data = new
    return data


def make_tables(length):
    slabs = length // LANES
    angle = np.array(slab_angles(slabs))[:, None] * np.arange(LANES)[None, :] / LANES
    twist = np.stack([np.cos(2 * np.pi * angle), np.sin(2 * np.pi * angle)], 1).astype(np.float32)
    grid = np.arange(LANES)[:, None] * np.arange(LANES)[None, :] % LANES * (2 * np.pi / LANES)
    cos, sin = np.cos(grid), np.sin(grid)
    fwd = np.block([[cos, -sin], [sin, cos]]).astype(np.float32)
    inv = np.block([[cos, sin], [-sin, cos]]).astype(np.float32)

    def two(mat):
        upper = mat.astype(jnp.bfloat16)
        lower = (mat - upper.astype(np.float32)).astype(jnp.bfloat16)
        return np.stack([upper, lower])

    return jnp.asarray(np.stack([twist, twist / length])), jnp.asarray(two(fwd)), jnp.asarray(two(inv))


def split_dot(value, mat_ref):
    upper = value.astype(jnp.bfloat16)
    lower = (value - upper.astype(jnp.float32)).astype(jnp.bfloat16)
    dot = lambda a, b: jnp.dot(a, b, preferred_element_type=jnp.float32)
    return dot(upper, mat_ref[0]) + (dot(lower, mat_ref[0]) + dot(upper, mat_ref[1]))


def forward_group(x_ref, row, twist_ref, mat_ref, work):
    parts, _, width = x_ref.shape
    per = width // LANES
    slabs = parts * per
    xs = [f32(x_ref[s // per, pl.ds(row, ROWS), s % per * LANES : (s % per + 1) * LANES]) for s in range(slabs)]
    for h in range(0, ROWS, HALF):
        data = slabs_forward([x[h : h + HALF] for x in xs])
        for j, (re, im) in enumerate(data):
            tc, ts = twist_ref[j, 0:1], twist_ref[j, 1:2]
            work[j * ROWS + h : j * ROWS + h + HALF, :LANES] = re * tc - im * ts
            work[j * ROWS + h : j * ROWS + h + HALF, LANES:] = re * ts + im * tc
    return split_dot(work[...], mat_ref)


def inverse_group(spec, twist_ref, mat_ref, work, store):
    slabs = spec.shape[0] // ROWS
    work[...] = split_dot(spec, mat_ref)
    for h in range(0, ROWS, HALF):
        data = []
        for j in range(slabs):
            tc, ts = twist_ref[j, 0:1], twist_ref[j, 1:2]
            re = work[j * ROWS + h : j * ROWS + h + HALF, :LANES]
            im = work[j * ROWS + h : j * ROWS + h + HALF, LANES:]
            data.append((re * tc + im * ts, im * tc - re * ts))
        for s, value in enumerate(slabs_inverse(data)):
            store(s, h, value)


def product(a, b):
    ar, ai, br, bi = a[:, :LANES], a[:, LANES:], b[:, :LANES], b[:, LANES:]
    return jnp.concatenate([ar * br - ai * bi, ar * bi + ai * br], 1)


def conj_product(a, b):
    ar, ai, br, bi = a[:, :LANES], a[:, LANES:], b[:, :LANES], b[:, LANES:]
    return jnp.concatenate([ar * br + ai * bi, ar * bi - ai * br], 1)


def spectrum_pair(filt_ref, gate_ref, row, twist_ref, fwd_ref, work):
    one = forward_group(filt_ref, row, twist_ref.at[0], fwd_ref, work.at[0])
    return one, forward_group(gate_ref, row, twist_ref.at[0], fwd_ref, work.at[1])


def put_slabs(out_ref, row, slabs_ref):
    per = out_ref.shape[2] // LANES
    for s in range(slabs_ref.shape[0]):
        lanes = slice(s % per * LANES, (s % per + 1) * LANES)
        out_ref[s // per, pl.ds(row, ROWS), lanes] = bf16(slabs_ref[s])


def storing(slabs_ref):
    def store(s, h, value):
        slabs_ref[s, h : h + HALF] = value

    return store


def span_of(per):
    return math.gcd(per, 2)


def over_groups(count, per, body, done):
    span = span_of(per)

    def step(i, carry):
        for g in range(per):
            body(g, pl.multiple_of((i * per + g) * ROWS, ROWS))
            if (g + 1) % span == 0:
                done(i * (per // span) + g // span)
        return carry

    lax.fori_loop(0, count // per, step, 0)


def column(cols_ref, rows, k):
    return cols_ref[rows, k : k + 1]


def tap(cols_ref, rows, branch, k):
    return column(cols_ref, rows, 3 * branch + k)


BIAS, GAIN = 9, 10


def after_wrap(now, before, steps):
    lanes = lax.broadcasted_iota(jnp.int32, now.shape, 1)
    return jnp.where(lanes < steps, before, now)


def short_slabs(x_ref, row, taps):
    parts, _, width = x_ref.shape
    per = width // LANES
    result, last = [], [0.0, 0.0]
    for s in range(parts * per):
        x = f32(x_ref[s // per, pl.ds(row, ROWS), s % per * LANES : (s % per + 1) * LANES])
        moved = [pltpu.roll(x, k, 1) for k in (1, 2)]
        one, two = (after_wrap(moved[k], last[k], k + 1) for k in range(2))
        result.append(bf16(taps[0] * x + taps[1] * one + taps[2] * two))
        last = moved
    return result


def convolve_kernel(pack_ref, cols_ref, twist_ref, fwd_ref, inv_ref, out_ref, spec_ref, gate_ref, token_ref, work, slabs, sent):
    chans = out_ref.shape[1]
    per = out_ref.shape[2] // LANES
    filt_ref, x1_ref, x2_ref = (pack_ref.at[:, k * chans : (k + 1) * chans] for k in range(3))

    def body(g, row):
        rows = pl.ds(row, ROWS)
        s1, s2 = (
            short_slabs(ref, row, [tap(cols_ref, rows, b, k) for k in range(3)]) for b, ref in ((1, x1_ref), (2, x2_ref))
        )
        for s, (one, two) in enumerate(zip(s1, s2)):
            gate_ref[s // per, rows, s % per * LANES : (s % per + 1) * LANES] = bf16(f32(one) * f32(two))
        filt, gate = spectrum_pair(filt_ref, gate_ref, row, twist_ref, fwd_ref, work.at[g])
        spec_ref[row // ROWS] = filt
        inverse_group(product(filt, gate), twist_ref.at[1], inv_ref, work.at[g, 0], storing(slabs.at[g]))
        put_slabs(out_ref, row, slabs.at[g])

    over_groups(chans // ROWS, work.shape[0], body, sent)
    token_ref[...] = jnp.zeros_like(token_ref)


def correlate_kernel(grad_ref, spec_ref, early_ref, twist_ref, fwd_ref, inv_ref, out_ref, work, slabs, sent):
    parts, chans, width = grad_ref.shape
    groups, per = chans // ROWS, work.shape[0]

    def body(g, row):
        grad = forward_group(grad_ref, row, twist_ref.at[0], fwd_ref, work.at[g, 0])
        mixed = conj_product(spec_ref[row // ROWS], grad)
        inverse_group(mixed, twist_ref.at[1], inv_ref, work.at[g, 0], storing(slabs.at[g]))
        put_slabs(out_ref, row, slabs.at[g])

    def done(i):
        for g in range(span_of(per)):
            sent(i * span_of(per) + g)

    over_groups(groups, per, body, done)
    for part in range(parts):
        sums = early_ref[:4, part * chans : (part + 1) * chans]
        upper = f32(bf16(sums))
        if part + 1 < parts:
            tips = to_rows([(0, 0), (1, 1), (2, 0), (3, 1)], out_ref[part + 1, :chans, :LANES])[:4]
        else:
            tips = jnp.zeros((4, chans), jnp.float32)
        rows = jnp.concatenate([tips, upper, sums - upper, jnp.zeros((4, chans), jnp.float32)], 0)
        rows = jnp.concatenate([rows, jnp.zeros((ROWS, width - chans), jnp.float32)], 1)
        out_ref[part, chans:] = bf16(rows)
    sent(groups)


def grads_kernel(back_ref, inner_ref, pack_ref, gate_ref, cols_ref, rows_ref, tiles, sent):
    parts, chans, _ = inner_ref.shape
    block = min(32, chans)
    for row in range(0, chans, block):
        rows = slice(row, row + block)
        taps = [[tap(cols_ref, rows, b, k) for k in range(3)] for b in range(3)]
        bias = column(cols_ref, rows, BIAS)
        totals, last = [None] * 7, [[None] * 2, [None] * 2]
        for part in range(parts):
            moved, shorts = [], []
            for b in (1, 2):
                x = f32(pack_ref[part, b * chans + row : b * chans + row + block])
                turns = [pltpu.roll(x, k, 1) for k in (1, 2)]
                fixed = []
                for k in range(2):
                    before = 0.0 if part == 0 else last[b - 1][k]
                    head = after_wrap(turns[k][:, :LANES], before, k + 1)
                    fixed.append(jnp.concatenate([head, turns[k][:, LANES:]], 1))
                    last[b - 1][k] = turns[k][:, :LANES]
                moved.append([x] + fixed)
                shorts.append(f32(bf16(taps[b][0] * x + taps[b][1] * fixed[0] + taps[b][2] * fixed[1])))
            inner = f32(inner_ref[part, rows])
            d_gated = f32(bf16(bias * inner + f32(back_ref[part, rows])))
            terms = []
            for b in (1, 2):
                g = f32(bf16(d_gated * shorts[2 - b]))
                terms += [fold(g * moved[b - 1][k]) for k in range(3)]
            terms.append(fold(inner * f32(gate_ref[part, rows])))
            totals = [t if total is None else total + t for total, t in zip(totals, terms)]
        for k in range(7):
            tiles[k, rows] = totals[k]
    rows_ref[...] = sum([sum_rows(k, tiles.at[k]) for k in range(7)])[:8]


def lags_kernel(gate_ref, grad_ref, twist_ref, fwd_ref, inv_ref, out_ref, token_ref, work, sent):
    chans = out_ref.shape[0]
    def body(g, row):
        def store(s, h, value):
            out_ref[pl.ds(pl.multiple_of(row + h, HALF), HALF), s * LANES : (s + 1) * LANES] = value

        gate, grad = spectrum_pair(gate_ref, grad_ref, row, twist_ref, fwd_ref, work.at[g])
        inverse_group(conj_product(gate, grad), twist_ref.at[1], inv_ref, work.at[g, 0], store)

    over_groups(chans // ROWS, work.shape[0], body, sent)
    token_ref[...] = jnp.zeros_like(token_ref)


def place(kernel, name, outs, args, scratch=(), flops=10**6, after=(), vmem=VMEM_MOST, lazy=()):
    n_args, n_outs = len(args), len(outs)
    drawn = [a[0] for a in lazy]
    far = [k for k in range(n_outs) if len(outs[k]) == 4]

    def body(*refs):
        out_refs = list(refs[n_args + len(after) :][:n_outs])
        rest = refs[n_args + len(after) + n_outs :]
        own, rest = rest[: len(scratch)], rest[len(scratch) :]
        stages, rest = rest[: len(far)], rest[len(far) :]
        sems, rest = rest[: len(far)], rest[len(far) :]
        held, waits = rest[: len(lazy)], rest[len(lazy) :]
        ins = list(refs[:n_args])

        def fetch(j, i):
            k, axis, pieces = lazy[j]
            size = args[k].shape[axis] // pieces
            start = i * size if isinstance(i, int) else pl.multiple_of(i * size, size)
            at = (slice(None),) * axis + (pl.ds(start, size),)
            return pltpu.make_async_copy(refs[k].at[at], held[j].at[at], waits[j].at[i])

        for i in range(max([a[2] for a in lazy], default=0)):
            for j in range(len(lazy)):
                if i < lazy[j][2]:
                    fetch(j, i).start()
        for j, k in enumerate(drawn):
            ins[k] = held[j]

        def need(i=None):
            for j in range(len(lazy)):
                if (i is None) == (lazy[j][2] == 1):
                    fetch(j, 0 if i is None else i).wait()


        def copy(j, i):
            axis, pieces = outs[far[j]][2:]
            size = outs[far[j]][0][axis] // pieces
            start = i * size if isinstance(i, int) else pl.multiple_of(i * size, size)
            at = (slice(None),) * axis + (pl.ds(start, size),)
            return pltpu.make_async_copy(stages[j].at[at], out_refs[far[j]].at[at], sems[j].at[i])

        def sent(i):
            for j in range(len(far)):
                copy(j, i).start()

        shown = list(out_refs)
        for j, k in enumerate(far):
            shown[k] = stages[j]
        more = {"need": need} if lazy else {}
        kernel(*ins, *shown, *own, sent=sent, **more)
        for j, k in enumerate(far):
            for i in range(outs[k][3]):
                copy(j, i).wait()

    near = pl.BlockSpec(memory_space=pltpu.VMEM)
    away = pl.BlockSpec(memory_space=pltpu.HBM)
    return pl.pallas_call(
        body,
        in_specs=[away if k in drawn else near for k in range(n_args)] + [away] * len(after),
        out_specs=[away if k in far else near for k in range(n_outs)],
        out_shape=[jax.ShapeDtypeStruct(*o[:2]) for o in outs],
        scratch_shapes=list(scratch)
        + [pltpu.VMEM(*outs[k][:2]) for k in far]
        + [pltpu.SemaphoreType.DMA((outs[k][3],)) for k in far]
        + [pltpu.VMEM(args[k].shape, args[k].dtype) for k in drawn]
        + [pltpu.SemaphoreType.DMA((a[2],)) for a in lazy],
        compiler_params=pltpu.CompilerParams(vmem_limit_bytes=vmem),
        cost_estimate=pl.CostEstimate(flops=flops, bytes_accessed=4 * 2**20, transcendentals=0),
        name=name,
    )(*args, *after)


TOKEN = ((8, LANES), jnp.float32)


def transforms(parts, chans, width):
    length = parts * width
    slabs = length // LANES
    groups = chans // ROWS
    per = math.gcd(groups, 4)
    tables = make_tables(length)
    work = pltpu.VMEM((per, 2, slabs * ROWS, 2 * LANES), jnp.float32)
    outs = pltpu.VMEM((per, slabs, ROWS, LANES), jnp.float32)
    flops = 2 * 3 * 4 * groups * slabs * ROWS * 256 * 256
    pieces = groups // span_of(per)
    result = ((parts, chans, width), jnp.bfloat16, 1, pieces)
    spec = ((groups, slabs * ROWS, 2 * LANES), jnp.float32, 0, pieces)

    longer = ((parts, chans + ROWS, width), jnp.bfloat16, 1, groups + 1)

    def convolve(pack, cols, after):
        args = (pack, cols, *tables)
        return place(convolve_kernel, "convolve", [result, spec, result, TOKEN], args, [work, outs], 3 * flops, after, VMEM_FFT)

    def correlate(grad, spec, early):
        args = (grad, spec, early, *tables)
        return place(correlate_kernel, "correlate", [longer], args, [work, outs], 2 * flops, vmem=VMEM_ALL)[0]

    def lags(gate, grad):
        out = ((chans, length), jnp.float32, 0, pieces)
        return place(lags_kernel, "lags", [out, TOKEN], (gate, grad, *tables), [work], 3 * flops)

    def grads(back, inner, pack, gate, cols):
        tiles = pltpu.VMEM((7, chans, LANES), jnp.float32)
        out = ((8, chans), jnp.float32)
        return place(grads_kernel, "grads", [out], (back, inner, pack, gate, cols), [tiles], flops)[0]

    return convolve, correlate, lags, grads


def picks(pairs):
    rows = lax.broadcasted_iota(jnp.int32, (ROWS, LANES), 0)
    lanes = lax.broadcasted_iota(jnp.int32, (ROWS, LANES), 1)
    hit = None
    for row, lane in pairs:
        here = (rows == row) & (lanes == lane)
        hit = here if hit is None else hit | here
    return hit.astype(jnp.float32).astype(jnp.bfloat16)


def to_rows(pairs, tile):
    return lax.dot_general(picks(pairs), tile, (((1,), (1,)), ((), ())), preferred_element_type=jnp.float32)


def to_lanes(pairs, rows):
    return lax.dot_general(rows, picks(pairs), (((0,), (0,)), ((), ())), preferred_element_type=jnp.float32)


def sum_rows(row, tile_ref):
    tile = tile_ref[...]
    upper = bf16(tile)
    lower = bf16(tile - f32(upper))
    ones = bf16((lax.broadcasted_iota(jnp.int32, (ROWS, LANES), 0) == row).astype(jnp.float32))
    dot = lambda v: lax.dot_general(ones, v, (((1,), (1,)), ((), ())), preferred_element_type=jnp.float32)
    return dot(upper) + dot(lower)


def fold(value):
    tile = value[:, :LANES]
    for k in range(1, value.shape[1] // LANES):
        tile = tile + value[:, k * LANES : (k + 1) * LANES]
    return tile


def fill_earlier(fill, slot, branch, edge):
    for steps in (1, 2):
        fill[slot, steps - 1] = to_lanes([(2 * branch + 2 - steps + i, i) for i in range(steps)], edge)


def fill_later(fill, slot, branch, edge):
    for steps in (1, 2):
        fill[slot, steps - 1] = to_lanes([(2 * branch + i, LANES - steps + i) for i in range(steps)], edge)


def earlier(value, fill, slot, rows, steps):
    moved = pltpu.roll(value, steps, 1)
    lanes = lax.broadcasted_iota(jnp.int32, (value.shape[0], LANES), 1)
    first = jnp.where(lanes < steps, fill[slot, steps - 1, rows], moved[:, :LANES])
    return jnp.concatenate([first, moved[:, LANES:]], 1)


def later(value, fill, slot, rows, steps):
    count = value.shape[1]
    moved = pltpu.roll(value, count - steps, 1)
    lanes = lax.broadcasted_iota(jnp.int32, (value.shape[0], LANES), 1)
    last = jnp.where(lanes >= LANES - steps, fill[slot, steps - 1, rows], moved[:, count - LANES :])
    return jnp.concatenate([moved[:, : count - LANES], last], 1)


def over_rows(ref, body, done=None, block=32, before=None):
    piece = ref.shape[0] // PARTS
    for row in range(0, ref.shape[0], block):
        if before and row % piece == 0:
            before(row // piece)
        body(slice(row, row + block))
        if done and (row + block) % piece == 0:
            done(row // piece)


def edge_kernel(x0_ref, x1_ref, x2_ref, edge_ref):
    total = None
    for b, ref in enumerate((x0_ref, x1_ref, x2_ref)):
        tile = ref[:, ref.shape[1] - LANES :]
        rows = to_rows([(2 * b, LANES - 2), (2 * b + 1, LANES - 1)], tile)
        total = rows if total is None else total + rows
    edge_ref[...] = bf16(total)


def gate_kernel(x0_ref, x1_ref, x2_ref, edge_ref, cols_ref, s0_ref, s1_ref, s2_ref, gated_ref, tips_ref, fill, sent):
    edge = edge_ref[...]
    for b in range(3):
        fill_earlier(fill, b, b, edge)

    def body(rows):
        shorts = []
        for b, (x_ref, s_ref) in enumerate(((x0_ref, s0_ref), (x1_ref, s1_ref), (x2_ref, s2_ref))):
            x = f32(x_ref[rows])
            total = tap(cols_ref, rows, b, 0) * x + tap(cols_ref, rows, b, 1) * earlier(x, fill, b, rows, 1)
            shorts.append(bf16(total + tap(cols_ref, rows, b, 2) * earlier(x, fill, b, rows, 2)))
            s_ref[rows] = shorts[b]
        gated_ref[rows] = bf16(f32(shorts[1]) * f32(shorts[2]))

    over_rows(gated_ref, body, sent)
    tips = to_rows([(0, 0), (1, 1)], s2_ref[:, :LANES]) + to_rows([(2, 0), (3, 1)], s1_ref[:, :LANES])
    tips_ref[...] = bf16(tips)


def mix(rows, conv_ref, s0_ref, gated_ref, cot_ref, cols_ref):
    inner = f32(conv_ref[rows]) + column(cols_ref, rows, BIAS) * f32(gated_ref[rows])
    return inner, f32(s0_ref[rows]) * inner, f32(cot_ref[rows])


def sums_kernel(conv_ref, s0_ref, gated_ref, cot_ref, cols_ref, out_ref, sent):
    lump = lambda v: jnp.sum(v.reshape(v.shape[0] // 8, 8, v.shape[1]), 0)
    total = [jnp.zeros((8, conv_ref.shape[1]), jnp.float32)] * 2

    def body(rows):
        _, mixed, cot = mix(rows, conv_ref, s0_ref, gated_ref, cot_ref, cols_ref)
        total[0] = total[0] + lump(mixed * mixed)
        total[1] = total[1] + lump(cot * column(cols_ref, rows, GAIN) * mixed)

    over_rows(conv_ref, body)

    for k in range(2):
        out_ref[k : k + 1] = jnp.sum(total[k], 0, keepdims=True)


def norm_terms(width, part_refs):
    total = part_refs[0][...]
    for ref in part_refs[1:]:
        total = total + ref[...]
    recip = lax.rsqrt(total[0:1] / width + EPS)
    return recip, recip * recip * recip * (total[1:2] / width)


def inner_kernel(width, n_ch, *refs, sent):
    parts, (conv_ref, s0_ref, gated_ref, cot_ref, cols_ref, out_ref) = refs[:n_ch], refs[n_ch:]
    recip, cubed = norm_terms(width, parts)

    def body(rows):
        _, mixed, cot = mix(rows, conv_ref, s0_ref, gated_ref, cot_ref, cols_ref)
        d_mixed = recip * (cot * column(cols_ref, rows, GAIN)) - mixed * cubed
        out_ref[rows] = bf16(d_mixed * f32(s0_ref[rows]))

    over_rows(out_ref, body, sent)


def output_kernel(width, n_ch, *refs, sent):
    parts, refs = refs[:n_ch], refs[n_ch:]
    conv_ref, s0_ref, gated_ref, cot_ref, cols_ref, x0_ref, edge_ref, inner_ref = refs[:8]
    out_ref, g0_ref, rows_ref, after_ref, fill, tiles = refs[8:]
    recip, cubed = norm_terms(width, parts)
    fill_earlier(fill, 0, 0, edge_ref[...])

    def body(rows):
        inner, mixed, cot = mix(rows, conv_ref, s0_ref, gated_ref, cot_ref, cols_ref)
        gain = column(cols_ref, rows, GAIN)
        normed = mixed * recip
        out_ref[rows] = bf16(normed * gain)
        g0 = bf16((recip * (cot * gain) - mixed * cubed) * inner)
        g0_ref[rows] = g0
        x, g = f32(x0_ref[rows]), f32(g0)
        tiles[0, rows] = fold(g * x)
        tiles[1, rows] = fold(g * earlier(x, fill, 0, rows, 1))
        tiles[2, rows] = fold(g * earlier(x, fill, 0, rows, 2))
        tiles[3, rows] = fold(cot * normed)

    over_rows(out_ref, body, sent)
    rows_ref[...] = sum([sum_rows(k, tiles.at[k]) for k in range(4)])[:8]
    after = to_rows([(0, 0), (1, 1), (2, 0), (3, 1)], inner_ref[:, :LANES])
    after_ref[...] = bf16(after + to_rows([(4, 0), (5, 1)], g0_ref[:, :LANES]))


def adjoint(g, branch, fill, slot, rows, cols_ref):
    total = tap(cols_ref, rows, branch, 0) * g + tap(cols_ref, rows, branch, 1) * later(g, fill, slot, rows, 1)
    return bf16(total + tap(cols_ref, rows, branch, 2) * later(g, fill, slot, rows, 2))


def first_kernel(g0_ref, edge_ref, cols_ref, out_ref, token_ref, fill, sent):
    fill_later(fill, 0, 2, edge_ref[...])

    def body(rows):
        out_ref[rows] = adjoint(f32(g0_ref[rows]), 0, fill, 0, rows, cols_ref)

    over_rows(out_ref, body, sent)
    token_ref[...] = jnp.zeros_like(token_ref)


def pair_kernel(
    back_ref, inner_ref, s1_ref, s2_ref, cols_ref, tips_ref, next_ref, bias_ref, grads_ref, d1_ref, d2_ref, *refs, sent, need
):
    short_ref, gain_ref, fill, edge = refs
    parts, longer, _ = back_ref.shape
    own = longer - ROWS
    sums = None
    for part in range(parts):
        lanes = slice(part * own, (part + 1) * own)
        extra = f32(back_ref[part, own:, :own])
        d_gated = f32(bf16(bias_ref[:, lanes] * f32(next_ref[:, lanes]) + extra))
        edge[:, lanes] = bf16(d_gated * f32(tips_ref[:, lanes]))
        terms = extra[4:8] + extra[8:12]
        sums = terms if sums is None else sums + terms
    for k in range(2):
        fill_later(fill, k, k, edge[...])
    short_ref[0] = sums[:3]
    short_ref[1] = grads_ref[:3]
    short_ref[2] = grads_ref[3:6]
    gain_ref[...] = sums[3:4]

    def body(rows):
        part, row = rows.start // own, rows.start % own
        back = f32(back_ref[part, row : row + rows.stop - rows.start])
        d_gated = f32(bf16(column(cols_ref, rows, BIAS) * f32(inner_ref[rows]) + back))
        for b, s_ref, d_ref in ((1, s2_ref, d1_ref), (2, s1_ref, d2_ref)):
            g = f32(bf16(d_gated * f32(s_ref[rows])))
            d_ref[rows] = adjoint(g, b, fill, b - 1, rows, cols_ref)

    over_rows(d1_ref, body, sent, min(32, own), need)


def exchange(value):
    return lax.all_to_all(value, "ctx", split_axis=0, concat_axis=0, tiled=True)


def local(x_first, x_second, x_value, short_filter, long_filter, skip_bias, norm_gain, cotangent):
    chans, steps_dev = x_first.shape
    n_ctx = lax.axis_size("ctx")
    n_ch = lax.axis_size("ch")
    width = chans * n_ch
    own = chans // n_ctx
    convolve, correlate, lags, grads = transforms(n_ctx, own, steps_dev)
    by_dev = lambda v: v.reshape(n_ctx, own, steps_dev)
    by_pos = lambda v: v.reshape(chans, steps_dev)

    array = ((chans, steps_dev), jnp.bfloat16, 0, PARTS)
    edges = ((ROWS, chans), jnp.bfloat16)
    rows8 = ((8, chans), jnp.float32)
    fills = lambda n: pltpu.VMEM((n, 2, chans, LANES), jnp.float32)
    tiles = lambda n: pltpu.VMEM((n, chans, LANES), jnp.float32)

    pack = exchange(jnp.concatenate([by_dev(v) for v in (long_filter, x_second, x_value)], 1))
    tip = pl.BlockSpec((chans, LANES), lambda i: (0, steps_dev // LANES - 1))
    edge = pl.pallas_call(
        edge_kernel,
        grid=(1,),
        in_specs=[tip] * 3,
        out_specs=pl.BlockSpec((ROWS, chans), lambda i: (0, 0)),
        out_shape=jax.ShapeDtypeStruct(*edges),
        name="edge",
    )(x_first, x_second, x_value)
    edge = shifted(edge, "ctx", 1)
    cols = jnp.concatenate([short_filter.reshape(9, chans), skip_bias[None], norm_gain[None]], 0)
    cols = jnp.pad(cols, ((0, ROWS - 11), (0, 0))).T
    own_cols = lax.dynamic_slice_in_dim(cols, lax.axis_index("ctx") * own, own, 0)
    conv_cm, filt_spec, gated_cm, conv_done = convolve(pack, own_cols, (edge,))
    first_s, second_s, third_s, gated, tips = place(
        gate_kernel, "gate", [array] * 4 + [edges], (x_first, x_second, x_value, edge, cols), [fills(3)], after=(conv_done,), vmem=VMEM_ALL
    )
    tips = shifted(tips, "ctx", -1)
    conv = by_pos(exchange(conv_cm))
    mix_args = (conv, first_s, gated, cotangent, cols)
    sums = place(sums_kernel, "sums", [((2, steps_dev), jnp.float32)], mix_args)[0]
    parts = [sums]
    for k in range(1, n_ch):
        parts.append(lax.ppermute(sums, "ch", [(i, i ^ k) for i in range(n_ch)]))
    inner_part = lambda *refs, sent: inner_kernel(width, n_ch, *refs, sent=sent)
    d_inner = place(inner_part, "inner", [array], (*parts, *mix_args))[0]
    d_inner_cm = exchange(by_dev(d_inner))
    output, grad_first, early_rows, after = place(
        lambda *refs, sent: output_kernel(width, n_ch, *refs, sent=sent),
        "output",
        [array, array, rows8, edges],
        (*parts, *mix_args, x_first, edge, d_inner),
        [fills(1), tiles(4)],
    )
    after = shifted(after, "ctx", -1)
    back_cm = correlate(d_inner_cm, filt_spec, early_rows)
    back = exchange(back_cm)
    d_first, first_done = place(first_kernel, "first", [array, TOKEN], (grad_first, after, cols), [fills(1)])
    own_rows = grads(back_cm, d_inner_cm, pack, gated_cm, own_cols)
    d_long, lags_done = lags(gated_cm, d_inner_cm)
    d_second, d_value, d_short, d_gain = place(
        pair_kernel,
        "pair",
        [array, array, ((3, 3, own), jnp.float32), ((1, own), jnp.float32)],
        (back, d_inner, second_s, third_s, cols, tips, after, skip_bias[None], own_rows),
        [fills(2), pltpu.VMEM(*edges)],
        after=(first_done, lags_done),
        lazy=[(1, 0, PARTS)],
    )
    return (output, d_first, d_second, d_value, d_long, d_short, own_rows[6], d_gain[0])


def solution(mesh):
    seq = P("ch", "ctx")
    own = ("ch", "ctx")
    return jax.shard_map(
        local,
        mesh=mesh,
        in_specs=(seq, seq, seq, P(None, None, "ch"), seq, P("ch"), P("ch"), seq),
        out_specs=(seq, seq, seq, seq, P(own, None), P(None, None, own), P(own), P(own)),
        check_vma=False,
    )
```
